256 devices in a mesh: gx: 4 (over x_hi, core), gy: 8 (over z), sa: 8 (over x_lo, y).
Axes of the slice: x: 4 (x_hi: 2, x_lo: 2; x = x_hi * 2 + x_lo), y: 4, z: 8, core: 2. Of those that a mesh axis runs over, the one named last changes fastest.
Arguments:
- green: bfloat16 [8, 16, 2, 2, 2048, 256], P('gx', 'gy', None, None, 'sa'), may hold values from -0.59765625 to 0.59765625
- offsets: int32 [4, 2], replicated, may hold values from -1 to 1, as said below
Outputs:
- hessian: float32 [8, 16, 4, 2, 256, 512], P('gx', 'gy', None, None, 'sa')
The draws below stay inside these ranges and needn't reach their ends.
Inputs may be any that keep to these rules, and one draw needn't show every extreme that they name: `offsets`: each row is an offset (dx, dy) within 1 tiles with dx >= 0, and dy >= 0 where dx = 0; rows are distinct; (1, -1) and (1, 1) are always among them.
All inputs are finite; a program needn't handle non-finite values.
Results may differ from the reference program's by a relative error of at most 0.0003.
Values may be sent and summed in bfloat16 or wider, within the bound.
No kernel may reach another device: no remote copies, remote signals or barrier semaphores. Data moves between devices by JAX's collectives and lax.ppermute only.
A program may use at most 128 MiB of HBM per device.

```python
import jax
import jax.numpy as jnp
from jax import lax

P_SIZE = 256
NF = 2
NPAIR = 4
TILES_X = 8
TILES_Y = 16
S = 2048


def draw_offsets(key, part):
    key = jax.random.fold_in(key, 7)
    loose = jnp.array([[0, 0], [0, 1], [1, 0]], jnp.int32)
    forced = jnp.array([[1, -1], [1, 1]], jnp.int32)
    picked = jax.random.permutation(key, 3)[:2]
    rows = jnp.concatenate([loose[picked], forced], axis=0)
    order = jax.random.permutation(jax.random.fold_in(key, 1), 4)
    return rows[order]


def level_of(stream_key, dims, cuts, least, top_value):
    def one(position, shards_of):
        draws = jax.random.uniform(jax.random.fold_in(jax.random.fold_in(stream_key, 6), position), (shards_of,), jnp.float32, least / len(cuts), top_value / len(cuts))
        return jnp.repeat(jnp.exp(draws), dims[position] // shards_of).reshape((-1,) + (1,) * (len(dims) - position - 1))

    factor_of = one(*cuts[0])
    for cut in cuts[1:]:
        factor_of = factor_of * one(*cut)
    return factor_of


def scatter_about(own_key, dims, spread, most, cuts=(), kind=jnp.bfloat16):
    gain = level_of(own_key, dims, cuts, -0.22, 0.18) if cuts else 1.0
    values = jax.random.normal(own_key, dims, jnp.float32) * spread * gain
    return jnp.minimum(jnp.maximum(values, -most), most).astype(kind)


def setup_inputs(seed: int = 0) -> dict:
    splits = jax.random.split(jax.random.key(seed), 3)
    green = scatter_about(splits[0], (TILES_X, TILES_Y, NF, 2, S, P_SIZE), 0.1, 0.59765625, ((0, 4), (1, 8), (4, 8)))
    offsets = draw_offsets(jax.random.fold_in(splits[2], 71), 0)
    return {"green": green, "offsets": offsets}


def pair_block(left, right):
    return lax.dot_general(left, right, (((0,), (0,)), ((), ())), preferred_element_type=jnp.float32)


def reference(green, offsets):
    padded = jnp.pad(green, ((1, 1), (1, 1), (0, 0), (0, 0), (0, 0), (0, 0)))
    zero = jnp.int32(0)

    def one_tile(flat):
        flat = flat.astype(jnp.int32)
        pos_x = flat // TILES_Y
        pos_y = flat % TILES_Y
        own = lax.dynamic_slice(green, (pos_x, pos_y, zero, zero, zero, zero), (1, 1, NF, 2, S, P_SIZE))
        left = own.reshape(NF, 2 * S, P_SIZE)
        blocks = []
        for index in range(NPAIR):
            start_x = (pos_x + 1 + offsets[index, 0]).astype(jnp.int32)
            start_y = (pos_y + 1 + offsets[index, 1]).astype(jnp.int32)
            beside = lax.dynamic_slice(padded, (start_x, start_y, zero, zero, zero, zero), (1, 1, NF, 2, S, P_SIZE))
            beside = beside.reshape(NF, 2, S, P_SIZE)
            real_rows = beside.reshape(NF, 2 * S, P_SIZE)
            imag_rows = jnp.concatenate([beside[:, 1], -beside[:, 0]], axis=1)
            right = jnp.concatenate([real_rows, imag_rows], axis=2)
            freq_blocks = [pair_block(left[freq], right[freq]) for freq in range(NF)]
            blocks.append(jnp.stack(freq_blocks, axis=0))
        return jnp.stack(blocks, axis=0)

    result = lax.map(one_tile, jnp.arange(TILES_X * TILES_Y, dtype=jnp.int32))
    return result.reshape(TILES_X, TILES_Y, NPAIR, NF, P_SIZE, 2 * P_SIZE)
```

```python
import functools

import jax
import jax.numpy as jnp
from jax import lax
from jax.experimental import pallas as pl
from jax.experimental.pallas import tpu as pltpu
from jax.sharding import PartitionSpec as P

NPAIR = 4
RING = 4
LOOSE0, LOOSE1, DOWN, UP = range(4)
GROUPS = (
    ((0, 0, LOOSE0), (0, 0, LOOSE1), (0, 0, UP), (1, 0, LOOSE0), (0, 1, DOWN)),
    ((0, 0, DOWN), (1, 0, LOOSE1), (1, 0, DOWN), (1, 0, UP), (0, 1, LOOSE0), (0, 1, LOOSE1)),
    ((0, 1, UP), (1, 1, LOOSE0), (1, 1, LOOSE1), (1, 1, DOWN), (1, 1, UP)),
)


def slot_table(offsets):
    dx = [offsets[k, 0] for k in range(NPAIR)]
    dy = [offsets[k, 1] for k in range(NPAIR)]
    code = [
        jnp.where(dx[k] == 0, dy[k], jnp.where(dy[k] == 0, 2, jnp.where(dy[k] < 0, 3, 4)))
        for k in range(NPAIR)
    ]
    rank = [
        sum((code[j] < code[k]).astype(jnp.int32) for j in range(NPAIR) if j != k) for k in range(NPAIR)
    ]

    def pick(values, slot):
        return sum(jnp.where(rank[k] == slot, values[k], 0) for k in range(NPAIR))

    return [(pick(dx, s), pick(dy, s), pick(list(range(NPAIR)), s)) for s in range(NPAIR)]


def blocks_kernel(groups, halo, *refs):
    count = 4 + (6 if halo else 0)
    meta, offsets, mine, theirs = refs[:4]
    outs = refs[count : count + 8 * len(groups)]
    left, right, acc = refs[count + 8 * len(groups) :]
    points = mine.shape[-1]
    traces = mine.shape[-2]
    sources = {(tx, ty): (mine.at[tx, ty], theirs.at[tx, ty]) for tx in range(2) for ty in range(2)}
    if halo:
        x_m, x_t, up_m, up_t, down_m, down_t = refs[4:count]
        for ty in range(2):
            sources[2, ty] = (x_m.at[ty], x_t.at[ty])
        for tx in range(3):
            sources[tx, 2] = (up_m.at[tx], up_t.at[tx])
        for tx in range(1, 3):
            sources[tx, -1] = (down_m.at[tx - 1], down_t.at[tx - 1])
    for (tx, ty), parts in sources.items():
        tile = tx * 4 + ty + 1
        for i, part in enumerate(parts):
            re, im = part[0], part[1]
            low = slice(2 * i * traces, (2 * i + 1) * traces)
            high = slice((2 * i + 1) * traces, (2 * i + 2) * traces)
            right[tile, low, :points] = re
            right[tile, high, :points] = im
            right[tile, low, points:] = im
            right[tile, high, points:] = -re
            if tx < 2 and 0 <= ty < 2:
                left[tx * 2 + ty, :, low] = re.T
                left[tx * 2 + ty, :, high] = im.T
    x_lo, y = meta[0], meta[1]
    slots = slot_table(offsets)
    rows = points // (2 * RING)
    step = 0
    for g, group in enumerate(groups):
        for b, (tx, ty, slot) in enumerate(group):
            dx, dy, _ = slots[slot]
            tile = (tx + dx) * 4 + (ty + dy + 1)
            place = acc.at[step % 2]
            step += 1
            place[...] = jnp.dot(left[tx * 2 + ty], right[tile], preferred_element_type=jnp.float32)
            for d in range(RING):
                for h in range(2):
                    start = lax.rem(x_lo + h, 2) * (points // 2) + lax.rem(y + d, RING) * rows
                    outs[8 * g + 2 * d + h][b] = place[pl.ds(pl.multiple_of(start, rows), rows), :]


def blocks(groups, meta, offsets, tiles, halos):
    points, traces = tiles[0].shape[-1], tiles[0].shape[-2]
    smem = pl.BlockSpec(memory_space=pltpu.SMEM)
    vmem = pl.BlockSpec(memory_space=pltpu.VMEM)
    out_shape = []
    for group in groups:
        shape = (len(group), points // (2 * RING), 2 * points)
        out_shape += [jax.ShapeDtypeStruct(shape, jnp.float32)] * (2 * RING)
    number = sum(len(group) for group in groups)
    outs = pl.pallas_call(
        functools.partial(blocks_kernel, groups, bool(halos)),
        out_shape=out_shape,
        in_specs=[smem, smem] + [vmem] * (len(tiles) + len(halos)),
        out_specs=[vmem] * len(out_shape),
        scratch_shapes=[
            pltpu.VMEM((4, points, 4 * traces), jnp.bfloat16),
            pltpu.VMEM((12, 4 * traces, 2 * points), jnp.bfloat16),
            pltpu.VMEM((2, points, 2 * points), jnp.float32),
        ],
        compiler_params=pltpu.CompilerParams(vmem_limit_bytes=40 * 1024 * 1024),
        cost_estimate=pl.CostEstimate(
            flops=number * 2 * points * 2 * points * 4 * traces,
            bytes_accessed=number * points * 2 * points * 4 + 4 * 1024 * 1024,
            transcendentals=0,
        ),
        name="tile_blocks",
    )(meta, offsets, *tiles, *halos)
    return [outs[8 * g : 8 * g + 8] for g in range(len(groups))]


def final_kernel(meta, offsets, *refs):
    out = refs[-1]
    x_lo = meta[0]
    slots = slot_table(offsets)
    for g, group in enumerate(GROUPS):
        own, before, after, other = refs[4 * g : 4 * g + 4]
        for b, (tx, ty, slot) in enumerate(group):
            pair = slots[slot][2]
            out[tx, ty, pair, x_lo] = own[b] + before[b] + after[b]
            out[tx, ty, pair, 1 - x_lo] = other[b]


def final(meta, offsets, parts, shape):
    smem = pl.BlockSpec(memory_space=pltpu.SMEM)
    vmem = pl.BlockSpec(memory_space=pltpu.VMEM)
    flat = [part for group in parts for part in group]
    return pl.pallas_call(
        final_kernel,
        out_shape=jax.ShapeDtypeStruct(shape, jnp.float32),
        in_specs=[smem, smem] + [vmem] * len(flat),
        out_specs=vmem,
        compiler_params=pltpu.CompilerParams(vmem_limit_bytes=40 * 1024 * 1024),
        name="place_blocks",
    )(meta, offsets, *flat)


def shift(axis, size, steps):
    return functools.partial(
        lax.ppermute, axis_name=axis, perm=[(i, i + steps) for i in range(size) if 0 <= i + steps < size]
    )


def per_device(green, offsets):
    points = green.shape[5]
    gx, gy = lax.axis_size("gx"), lax.axis_size("gy")
    sa = lax.axis_index("sa")
    x_lo, y = sa // RING, sa % RING
    meta = jnp.stack([x_lo, y]).astype(jnp.int32)
    swap = functools.partial(lax.ppermute, axis_name="sa", perm=[(i, (i + RING) % (2 * RING)) for i in range(2 * RING)])

    def around(steps):
        perm = [(h * RING + i, h * RING + (i + steps) % RING) for h in range(2) for i in range(RING)]
        return functools.partial(lax.ppermute, axis_name="sa", perm=perm)

    def halo(tiles):
        beside = shift("gx", gx, -1)(tiles[0])
        up = shift("gy", gy, -1)(jnp.stack([tiles[0, 0], tiles[1, 0], beside[0]]))
        down = shift("gy", gy, 1)(jnp.stack([tiles[1, 1], beside[1]]))
        return beside, up, down

    theirs = swap(lax.dynamic_index_in_dim(green, 1 - x_lo, 2, keepdims=False))
    mine = lax.dynamic_index_in_dim(green, x_lo, 2, keepdims=False)
    halo_mine = halo(mine)
    halo_theirs = halo(theirs)
    tiles = [mine, theirs]
    halos = [value for pair in zip(halo_mine, halo_theirs) for value in pair]
    pieces = blocks(GROUPS[:1], meta, offsets, tiles, []) + blocks(GROUPS[1:], meta, offsets, tiles, halos)
    parts = []
    for own_a, own_b, next_a, next_b, far_a, far_b, prev_a, prev_b in pieces:
        far_b = around(-1)(far_b)
        far_a = around(1)(far_a)
        from_prev_b = around(1)(next_b)
        from_next_a = around(-1)(prev_a)
        from_next_b = around(-1)(prev_b + far_b)
        from_prev_a = around(1)(next_a + far_a)
        other = swap(own_b + from_prev_b + from_next_b)
        parts.append((own_a, from_prev_a, from_next_a, other))
    shape = green.shape[:2] + (NPAIR, green.shape[2], points // (2 * RING), 2 * points)
    return final(meta, offsets, parts, shape)


def solution(mesh):
    return jax.shard_map(
        per_device,
        mesh=mesh,
        in_specs=(P("gx", "gy", None, None, "sa", None), P()),
        out_specs=P("gx", "gy", None, None, "sa", None),
        check_vma=False,
    )
```

```python
import functools

import jax
import jax.numpy as jnp
from jax import lax
from jax.experimental import pallas as pl
from jax.experimental.pallas import tpu as pltpu
from jax.sharding import PartitionSpec as P

NPAIR = 4
RING = 4
LOOSE0, LOOSE1, DOWN, UP = range(4)
SHORT = pl.CostEstimate(flops=0, bytes_accessed=0, transcendentals=0)
EARLY = ((0, 0, UP), (0, 0, LOOSE0), (0, 0, LOOSE1), (0, 1, DOWN), (1, 0, LOOSE0))
SIDES = (
    (0, 0, DOWN),
    (1, 0, LOOSE1),
    (1, 0, UP),
    (0, 1, LOOSE0),
    (0, 1, LOOSE1),
    (0, 1, UP),
)
CORNERS = ((1, 1, LOOSE0), (1, 1, LOOSE1), (1, 1, DOWN), (1, 1, UP), (1, 0, DOWN))
BESIDE = ((2, 0), (2, 1))
ABOVE = ((0, 2), (1, 2))
BELOW = ((1, -1),)
CORNER_UP = ((2, 2),)
CORNER_DOWN = ((2, -1),)


def slot_table(offsets):
    dx = [offsets[k, 0] for k in range(NPAIR)]
    dy = [offsets[k, 1] for k in range(NPAIR)]
    code = [
        jnp.where(dx[k] == 0, dy[k], jnp.where(dy[k] == 0, 2, jnp.where(dy[k] < 0, 3, 4)))
        for k in range(NPAIR)
    ]
    rank = [
        sum((code[j] < code[k]).astype(jnp.int32) for j in range(NPAIR) if j != k) for k in range(NPAIR)
    ]

    def pick(values, slot):
        return sum(jnp.where(rank[k] == slot, values[k], 0) for k in range(NPAIR))

    return [(pick(dx, s), pick(dy, s), pick(list(range(NPAIR)), s)) for s in range(NPAIR)]


def store_pieces(outs, place, meta, index, count):
    own_a, own_b, up_first, down_first, up_second, down_second = outs
    x_lo, y = meta[0], meta[1]
    half = place.shape[0] // 2
    rows = half // RING
    target = {
        (0, 0): (own_a, 0),
        (0, 1): (own_b, 0),
        (2, 0): (up_first, 0),
        (1, 1): (up_first, count),
        (2, 1): (down_first, 0),
        (3, 0): (down_first, count),
        (1, 0): (up_second, 0),
        (3, 1): (down_second, 0),
    }
    for (d, h), (ref, base) in target.items():
        start = lax.rem(x_lo + h, 2) * half + lax.rem(y + d, RING) * rows
        ref[base + index] = place[pl.ds(pl.multiple_of(start, rows), rows), :]


def load_tile(left, right, tile, own, parts):
    traces, points = parts[0].shape[-2:]
    for i, part in enumerate(parts):
        re, im = part[0], part[1]
        low = slice(2 * i * traces, (2 * i + 1) * traces)
        high = slice((2 * i + 1) * traces, (2 * i + 2) * traces)
        right[tile, low, :points] = re
        right[tile, high, :points] = im
        right[tile, low, points:] = im
        right[tile, high, points:] = -re
        if own is not None:
            left[own, :, low] = re.T
            left[own, :, high] = im.T


def early_kernel(meta, offsets, token, green, *refs):
    outs, (left, right, acc) = refs[:6], refs[7:]
    refs[6][...] = token[...]
    slots = slot_table(offsets)
    count = 2 * len(EARLY)
    for freq in range(2):
        for tx in range(2):
            for ty in range(2):
                load_tile(left, right, freq * 8 + tx * 4 + ty + 1, freq * 4 + tx * 2 + ty, [green.at[tx, ty, freq]])
    for b, (tx, ty, slot) in enumerate(EARLY):
        dx, dy, _ = slots[slot]
        for freq in range(2):
            place = acc.at[freq]
            tile = freq * 8 + (tx + dx) * 4 + (ty + dy + 1)
            place[...] = jnp.dot(left[freq * 4 + tx * 2 + ty], right[tile], preferred_element_type=jnp.float32)
            store_pieces(outs, place, meta, 2 * b + freq, count)


def late_kernel(group, where, *refs):
    count = 3 + len(where)
    meta, offsets, token = refs[:3]
    outs, (left, right, acc) = refs[count : count + 6], refs[count + 7 :]
    refs[count + 6][...] = token[...]
    sources = {}
    for ref, tiles in zip(refs[3:count], where):
        for i, (tx, ty) in enumerate(tiles):
            sources.setdefault((tx, ty), []).append(ref.at[i])
    for (tx, ty), parts in sources.items():
        own = tx * 2 + ty if tx < 2 and 0 <= ty < 2 else None
        load_tile(left, right, tx * 4 + ty + 1, own, parts)
    slots = slot_table(offsets)
    for b, (tx, ty, slot) in enumerate(group):
        dx, dy, _ = slots[slot]
        tile = (tx + dx) * 4 + (ty + dy + 1)
        place = acc.at[b % 2]
        place[...] = jnp.dot(left[tx * 2 + ty], right[tile], preferred_element_type=jnp.float32)
        store_pieces(outs, place, meta, b, len(group))


def call_blocks(kernel, count, depth, tiles, lefts, points, arrays, token, name):
    meta, offsets, *values = arrays
    smem = pl.BlockSpec(memory_space=pltpu.SMEM)
    vmem = pl.BlockSpec(memory_space=pltpu.VMEM)
    *pieces, token = pl.pallas_call(
        kernel,
        out_shape=[
            jax.ShapeDtypeStruct((pieces * count, points // (2 * RING), 2 * points), jnp.float32)
            for pieces in (1, 1, 2, 2, 1, 1)
        ]
        + [jax.ShapeDtypeStruct(token.shape, token.dtype)],
        in_specs=[smem, smem] + [vmem] * (1 + len(values)),
        out_specs=[vmem] * 7,
        scratch_shapes=[
            pltpu.VMEM((lefts, points, depth), jnp.bfloat16),
            pltpu.VMEM((tiles, depth, 2 * points), jnp.bfloat16),
            pltpu.VMEM((2, points, 2 * points), jnp.float32),
        ],
        compiler_params=pltpu.CompilerParams(vmem_limit_bytes=40 * 1024 * 1024),
        cost_estimate=SHORT,
        name=name,
    )(meta, offsets, token, *values)
    return pieces, token


def call_step(kernel, out_shape, token, arrays, name):
    vmem = pl.BlockSpec(memory_space=pltpu.VMEM)
    *outs, token = pl.pallas_call(
        kernel,
        out_shape=list(out_shape) + [jax.ShapeDtypeStruct(token.shape, token.dtype)],
        in_specs=[vmem] * (1 + len(arrays)),
        out_specs=[vmem] * (1 + len(out_shape)),
        cost_estimate=SHORT,
        name=name,
    )(token, *arrays)
    return outs, token


def swapped_kernel(token, mine, theirs, above_mine, beside, below, above_theirs, out_token):
    for i, part in enumerate((mine, theirs)):
        beside[i] = part[0]
        below[i] = part[1, 1]
    for tx in range(2):
        above_theirs[tx] = theirs[tx, 0]
    out_token[...] = token[...]


def second_kernel(token, up_received, down_received, up_own, down_own, *refs):
    up, down, out_token = refs[-3:]
    count = up_own.shape[0]
    up[...] = up_own[...] + up_received[:count]
    down[...] = down_own[...] + down_received[:count]
    out_token[...] = token[...]


def back_kernel(token, down_arrived, own, up_received, *refs):
    out, out_token = refs[-2:]
    count = own.shape[0]
    out[...] = own[...] + up_received[count:] + down_arrived[...]
    out_token[...] = token[...]


def final_kernel(meta, offsets, *refs):
    out = refs[-1]
    x_lo = meta[0]
    slots = slot_table(offsets)
    for g, group in enumerate((EARLY, SIDES, CORNERS)):
        own, before, after, other = refs[4 * g : 4 * g + 4]
        for b, (tx, ty, slot) in enumerate(group):
            pair = slots[slot][2]
            if g == 0:
                for freq in range(2):
                    i = 2 * b + freq
                    out[tx, ty, pair, freq] = (own[i] + before[i] + after[len(group) * 2 + i]) + other[i]
            else:
                out[tx, ty, pair, x_lo] = own[b] + before[b] + after[len(group) + b]
                out[tx, ty, pair, 1 - x_lo] = other[b]


def final(meta, offsets, parts, token, shape):
    smem = pl.BlockSpec(memory_space=pltpu.SMEM)
    vmem = pl.BlockSpec(memory_space=pltpu.VMEM)
    flat = [part for group in parts for part in group]
    return pl.pallas_call(
        final_kernel,
        out_shape=jax.ShapeDtypeStruct(shape, jnp.float32),
        in_specs=[smem, smem] + [vmem] * (len(flat) + 1),
        out_specs=vmem,
        compiler_params=pltpu.CompilerParams(vmem_limit_bytes=40 * 1024 * 1024),
        name="place_blocks",
    )(meta, offsets, *flat, token)


def per_device(green, offsets):
    points, traces = green.shape[5], green.shape[4]
    gx, gy = lax.axis_size("gx"), lax.axis_size("gy")
    sa = lax.axis_index("sa")
    x_lo, y = sa // RING, sa % RING
    meta = jnp.stack([x_lo, y]).astype(jnp.int32)

    def swap(value):
        return lax.ppermute(value, "sa", [(i, (i + RING) % (2 * RING)) for i in range(2 * RING)])

    def around(value, steps):
        return lax.ppermute(value, "sa", [(h * RING + i, h * RING + (i + steps) % RING) for h in range(2) for i in range(RING)])

    def tiles_from(value, dx, dy):
        perm = [
            ((ix + dx) * gy + iy + dy, ix * gy + iy)
            for ix in range(gx - dx)
            for iy in range(max(0, -dy), min(gy, gy - dy))
        ]
        return lax.ppermute(value, ("gx", "gy"), perm)

    def first(pieces):
        return around(pieces[2], 1), around(pieces[3], -1)

    def second(pieces, received, token, also=()):
        up, down = pieces[4], pieces[5]
        (up, down), token = call_step(second_kernel, [up, down], token, [*received, up, down, *also], "second")
        return (around(up, 1), around(down, -1)), token

    def back(pieces, received, arrived, token):
        own = pieces[1]
        (out,), token = call_step(back_kernel, [own], token, [arrived[1], own, received[0], arrived[0]], "back")
        return swap(out), token

    def blocks(group, inputs, token, name):
        kernel = functools.partial(late_kernel, group, [where for where, _ in inputs])
        arrays = [meta, offsets] + [value for _, value in inputs]
        return call_blocks(kernel, len(group), 4 * traces, 12, 4, points, arrays, token, name)

    token = jnp.zeros((8, 128), jnp.float32)
    theirs = swap(lax.dynamic_index_in_dim(green, 1 - x_lo, 2, keepdims=False))
    mine = lax.dynamic_index_in_dim(green, x_lo, 2, keepdims=False)
    above_mine = tiles_from(mine[:, 0], 0, 1)
    early, token = call_blocks(
        early_kernel, 2 * len(EARLY), 2 * traces, 16, 8, points, [meta, offsets, green], token, "early_blocks"
    )
    early_first = first(early)
    dtype, shape = green.dtype, mine.shape[2:]
    sent = [jax.ShapeDtypeStruct(lead + shape, dtype) for lead in ((2, 2), (2,), (2,))]
    sent, token = call_step(swapped_kernel, sent, token, [mine, theirs, above_mine], "swapped")
    above_theirs = tiles_from(sent[2], 0, 1)
    beside = tiles_from(sent[0], 1, 0)
    below = tiles_from(sent[1], 0, -1)
    corner_up = tiles_from(beside[:, 0], 0, 1)
    corner_down = tiles_from(beside[:, 1], 0, -1)
    own = ((0, 0), (0, 1), (1, 0), (1, 1))
    tiles = [(own, mine.reshape(4, *shape)), (own, theirs.reshape(4, *shape))]
    early_second, token = second(early, early_first, token)
    tiles += [(BESIDE, beside[0]), (BESIDE, beside[1]), (BELOW, below[:1]), (BELOW, below[1:])]
    tiles += [(ABOVE, above_mine), (ABOVE, above_theirs)]
    sides, token = blocks(SIDES, tiles, token, "side_blocks")
    sides_first = first(sides)
    early_back, token = back(early, early_first, early_second, token)
    tiles += [(CORNER_UP, corner_up[:1]), (CORNER_UP, corner_up[1:])]
    tiles += [(CORNER_DOWN, corner_down[:1]), (CORNER_DOWN, corner_down[1:])]
    corners, token = blocks(CORNERS, tiles, token, "corner_blocks")
    corners_first = first(corners)
    sides_second, token = second(sides, sides_first, token, [early_back])
    corners_second, token = second(corners, corners_first, token)
    sides_back, token = back(sides, sides_first, sides_second, token)
    corners_back, token = back(corners, corners_first, corners_second, token)
    parts = [
        (early[0], early_second[0], early_first[1], early_back),
        (sides[0], sides_second[0], sides_first[1], sides_back),
        (corners[0], corners_second[0], corners_first[1], corners_back),
    ]
    shape = green.shape[:2] + (NPAIR, green.shape[2], points // (2 * RING), 2 * points)
    return final(meta, offsets, parts, token, shape)


def solution(mesh):
    return jax.shard_map(
        per_device,
        mesh=mesh,
        in_specs=(P("gx", "gy", None, None, "sa", None), P()),
        out_specs=P("gx", "gy", None, None, "sa", None),
        check_vma=False,
    )
```

```python
import functools

import jax
import jax.numpy as jnp
from jax import lax
from jax.experimental import pallas as pl
from jax.experimental.pallas import tpu as pltpu
from jax.sharding import PartitionSpec as P

NPAIR = 4
RING = 4
LOOSE0, LOOSE1, DOWN, UP = range(4)
MIB = 1024 * 1024
EARLY = ((0, 0, UP), (0, 0, LOOSE0), (0, 0, LOOSE1), (0, 1, DOWN), (1, 0, LOOSE0))
SIDES = (
    (0, 0, DOWN),
    (1, 0, LOOSE1),
    (1, 0, UP),
    (0, 1, LOOSE0),
    (0, 1, LOOSE1),
    (0, 1, UP),
)
CORNERS = ((1, 1, LOOSE0), (1, 1, LOOSE1), (1, 1, DOWN), (1, 1, UP), (1, 0, DOWN))
BESIDE = ((2, 0), (2, 1))
ABOVE = ((0, 2), (1, 2))
BELOW = ((1, -1),)
CORNER_UP = ((2, 2),)
CORNER_DOWN = ((2, -1),)


def slot_table(offsets):
    dx = [offsets[k, 0] for k in range(NPAIR)]
    dy = [offsets[k, 1] for k in range(NPAIR)]
    code = [
        jnp.where(dx[k] == 0, dy[k], jnp.where(dy[k] == 0, 2, jnp.where(dy[k] < 0, 3, 4)))
        for k in range(NPAIR)
    ]
    rank = [
        sum((code[j] < code[k]).astype(jnp.int32) for j in range(NPAIR) if j != k) for k in range(NPAIR)
    ]

    def pick(values, slot):
        return sum(jnp.where(rank[k] == slot, values[k], 0) for k in range(NPAIR))

    return [(pick(dx, s), pick(dy, s), pick(list(range(NPAIR)), s)) for s in range(NPAIR)]


def store_pieces(outs, place, meta, index, count):
    own_a, own_b, up_first, down_first, up_second, down_second = outs
    x_lo, y = meta[0], meta[1]
    half = place.shape[0] // 2
    rows = half // RING
    target = {
        (0, 0): (own_a, 0),
        (0, 1): (own_b, 0),
        (2, 0): (up_first, 0),
        (1, 1): (up_first, count),
        (2, 1): (down_first, 0),
        (3, 0): (down_first, count),
        (1, 0): (up_second, 0),
        (3, 1): (down_second, 0),
    }
    for (d, h), (ref, base) in target.items():
        start = lax.rem(x_lo + h, 2) * half + lax.rem(y + d, RING) * rows
        ref[base + index] = place[pl.ds(pl.multiple_of(start, rows), rows), :]


def load_tile(left, right, tile, own, parts):
    traces, points = parts[0].shape[-2:]
    for i, part in enumerate(parts):
        re, im = part[0], part[1]
        low = slice(2 * i * traces, (2 * i + 1) * traces)
        high = slice((2 * i + 1) * traces, (2 * i + 2) * traces)
        right[tile, low, :points] = re
        right[tile, high, :points] = im
        right[tile, low, points:] = im
        right[tile, high, points:] = -re
        if own is not None:
            left[own, :, low] = re.T
            left[own, :, high] = im.T


def early_kernel(meta, offsets, token, green, *refs):
    outs, (left, right, acc) = refs[:6], refs[7:]
    refs[6][...] = token[...]
    slots = slot_table(offsets)
    count = 2 * len(EARLY)
    for freq in range(2):
        for tx in range(2):
            for ty in range(2):
                load_tile(left, right, freq * 8 + tx * 4 + ty + 1, freq * 4 + tx * 2 + ty, [green.at[tx, ty, freq]])
    for b, (tx, ty, slot) in enumerate(EARLY):
        dx, dy, _ = slots[slot]
        for freq in range(2):
            place = acc.at[freq]
            tile = freq * 8 + (tx + dx) * 4 + (ty + dy + 1)
            place[...] = jnp.dot(left[freq * 4 + tx * 2 + ty], right[tile], preferred_element_type=jnp.float32)
            store_pieces(outs, place, meta, 2 * b + freq, count)


def late_kernel(group, where, *refs):
    count = 3 + len(where)
    meta, offsets, token = refs[:3]
    outs, (left, right, acc) = refs[count : count + 6], refs[count + 7 :]
    refs[count + 6][...] = token[...]
    sources = {}
    for ref, tiles in zip(refs[3:count], where):
        for i, (tx, ty) in enumerate(tiles):
            sources.setdefault((tx, ty), []).append(ref.at[i])
    for (tx, ty), parts in sources.items():
        own = tx * 2 + ty if tx < 2 and 0 <= ty < 2 else None
        load_tile(left, right, tx * 4 + ty + 1, own, parts)
    slots = slot_table(offsets)
    for b, (tx, ty, slot) in enumerate(group):
        dx, dy, _ = slots[slot]
        tile = (tx + dx) * 4 + (ty + dy + 1)
        place = acc.at[b % 2]
        place[...] = jnp.dot(left[tx * 2 + ty], right[tile], preferred_element_type=jnp.float32)
        store_pieces(outs, place, meta, b, len(group))


def call_blocks(kernel, count, depth, tiles, lefts, points, arrays, token, name):
    meta, offsets, *values = arrays
    smem = pl.BlockSpec(memory_space=pltpu.SMEM)
    vmem = pl.BlockSpec(memory_space=pltpu.VMEM)
    *pieces, token = pl.pallas_call(
        kernel,
        out_shape=[
            jax.ShapeDtypeStruct((pieces * count, points // (2 * RING), 2 * points), jnp.float32)
            for pieces in (1, 1, 2, 2, 1, 1)
        ]
        + [jax.ShapeDtypeStruct(token.shape, token.dtype)],
        in_specs=[smem, smem] + [vmem] * (1 + len(values)),
        out_specs=[vmem] * 7,
        scratch_shapes=[
            pltpu.VMEM((lefts, points, depth), jnp.bfloat16),
            pltpu.VMEM((tiles, depth, 2 * points), jnp.bfloat16),
            pltpu.VMEM((2, points, 2 * points), jnp.float32),
        ],
        compiler_params=pltpu.CompilerParams(vmem_limit_bytes=(24 if len(values) > 1 else 18) * MIB),
        cost_estimate=pl.CostEstimate(flops=0, bytes_accessed=8 * MIB, transcendentals=0),
        name=name,
    )(meta, offsets, token, *values)
    return pieces, token


def call_step(kernel, out_shape, token, arrays, name):
    vmem = pl.BlockSpec(memory_space=pltpu.VMEM)
    *outs, token = pl.pallas_call(
        kernel,
        out_shape=list(out_shape) + [jax.ShapeDtypeStruct(token.shape, token.dtype)],
        in_specs=[vmem] * (1 + len(arrays)),
        out_specs=[vmem] * (1 + len(out_shape)),
        compiler_params=pltpu.CompilerParams(vmem_limit_bytes=6 * MIB),
        cost_estimate=pl.CostEstimate(flops=0, bytes_accessed=4 * MIB, transcendentals=0),
        name=name,
    )(token, *arrays)
    return outs, token


def swapped_kernel(token, mine, theirs, above_mine, beside, below, above_theirs, out_token):
    for i, part in enumerate((mine, theirs)):
        beside[i] = part[0]
        below[i] = part[1, 1]
    for tx in range(2):
        above_theirs[tx] = theirs[tx, 0]
    out_token[...] = token[...]


def second_kernel(token, up_received, down_received, up_own, down_own, *refs):
    up, down, out_token = refs[-3:]
    count = up_own.shape[0]
    up[...] = up_own[...] + up_received[:count]
    down[...] = down_own[...] + down_received[:count]
    out_token[...] = token[...]


def back_kernel(token, down_arrived, own, up_received, *refs):
    out, out_token = refs[-2:]
    count = own.shape[0]
    out[...] = own[...] + up_received[count:] + down_arrived[...]
    out_token[...] = token[...]


def final_kernel(meta, offsets, *refs):
    out = refs[-1]
    x_lo = meta[0]
    slots = slot_table(offsets)
    for g, group in enumerate((EARLY, SIDES, CORNERS)):
        own, before, after, other = refs[4 * g : 4 * g + 4]
        for b, (tx, ty, slot) in enumerate(group):
            pair = slots[slot][2]
            if g == 0:
                for freq in range(2):
                    i = 2 * b + freq
                    out[tx, ty, pair, freq] = (own[i] + before[i] + after[len(group) * 2 + i]) + other[i]
            else:
                out[tx, ty, pair, x_lo] = own[b] + before[b] + after[len(group) + b]
                out[tx, ty, pair, 1 - x_lo] = other[b]


def final(meta, offsets, parts, token, shape):
    smem = pl.BlockSpec(memory_space=pltpu.SMEM)
    vmem = pl.BlockSpec(memory_space=pltpu.VMEM)
    flat = [part for group in parts for part in group]
    return pl.pallas_call(
        final_kernel,
        out_shape=jax.ShapeDtypeStruct(shape, jnp.float32),
        in_specs=[smem, smem] + [vmem] * (len(flat) + 1),
        out_specs=vmem,
        compiler_params=pltpu.CompilerParams(vmem_limit_bytes=10 * MIB),
        cost_estimate=pl.CostEstimate(flops=0, bytes_accessed=8 * MIB, transcendentals=0),
        name="place_blocks",
    )(meta, offsets, *flat, token)


def per_device(green, offsets):
    points, traces = green.shape[5], green.shape[4]
    gx, gy = lax.axis_size("gx"), lax.axis_size("gy")
    sa = lax.axis_index("sa")
    x_lo, y = sa // RING, sa % RING
    meta = jnp.stack([x_lo, y]).astype(jnp.int32)

    def swap(value):
        return lax.ppermute(value, "sa", [(i, (i + RING) % (2 * RING)) for i in range(2 * RING)])

    def around(value, steps):
        return lax.ppermute(value, "sa", [(h * RING + i, h * RING + (i + steps) % RING) for h in range(2) for i in range(RING)])

    def tiles_from(value, dx, dy):
        perm = [
            ((ix + dx) * gy + iy + dy, ix * gy + iy)
            for ix in range(gx - dx)
            for iy in range(max(0, -dy), min(gy, gy - dy))
        ]
        return lax.ppermute(value, ("gx", "gy"), perm)

    def first(pieces):
        return around(pieces[2], 1), around(pieces[3], -1)

    def second(pieces, received, token, also=()):
        up, down = pieces[4], pieces[5]
        (up, down), token = call_step(second_kernel, [up, down], token, [*received, up, down, *also], "second")
        return (around(up, 1), around(down, -1)), token

    def back(pieces, received, arrived, token):
        own = pieces[1]
        (out,), token = call_step(back_kernel, [own], token, [arrived[1], own, received[0], arrived[0]], "back")
        return swap(out), token

    def blocks(group, inputs, token, name):
        kernel = functools.partial(late_kernel, group, [where for where, _ in inputs])
        arrays = [meta, offsets] + [value for _, value in inputs]
        return call_blocks(kernel, len(group), 4 * traces, 12, 4, points, arrays, token, name)

    token = jnp.zeros((8, 128), jnp.float32)
    theirs = swap(lax.dynamic_index_in_dim(green, 1 - x_lo, 2, keepdims=False))
    mine = lax.dynamic_index_in_dim(green, x_lo, 2, keepdims=False)
    above_mine = tiles_from(mine[:, 0], 0, 1)
    early, token = call_blocks(
        early_kernel, 2 * len(EARLY), 2 * traces, 16, 8, points, [meta, offsets, green], token, "early_blocks"
    )
    early_first = first(early)
    dtype, shape = green.dtype, mine.shape[2:]
    sent = [jax.ShapeDtypeStruct(lead + shape, dtype) for lead in ((2, 2), (2,), (2,))]
    sent, token = call_step(swapped_kernel, sent, token, [mine, theirs, above_mine], "swapped")
    above_theirs = tiles_from(sent[2], 0, 1)
    beside = tiles_from(sent[0], 1, 0)
    below = tiles_from(sent[1], 0, -1)
    corner_up = tiles_from(beside[:, 0], 0, 1)
    corner_down = tiles_from(beside[:, 1], 0, -1)
    own = ((0, 0), (0, 1), (1, 0), (1, 1))
    tiles = [(own, mine.reshape(4, *shape)), (own, theirs.reshape(4, *shape))]
    early_second, token = second(early, early_first, token)
    tiles += [(BESIDE, beside[0]), (BESIDE, beside[1]), (BELOW, below[:1]), (BELOW, below[1:])]
    tiles += [(ABOVE, above_mine), (ABOVE, above_theirs)]
    sides, token = blocks(SIDES, tiles, token, "side_blocks")
    sides_first = first(sides)
    early_back, token = back(early, early_first, early_second, token)
    tiles += [(CORNER_UP, corner_up[:1]), (CORNER_UP, corner_up[1:])]
    tiles += [(CORNER_DOWN, corner_down[:1]), (CORNER_DOWN, corner_down[1:])]
    corners, token = blocks(CORNERS, tiles, token, "corner_blocks")
    corners_first = first(corners)
    sides_second, token = second(sides, sides_first, token, [early_back])
    corners_second, token = second(corners, corners_first, token)
    sides_back, token = back(sides, sides_first, sides_second, token)
    corners_back, token = back(corners, corners_first, corners_second, token)
    parts = [
        (early[0], early_second[0], early_first[1], early_back),
        (sides[0], sides_second[0], sides_first[1], sides_back),
        (corners[0], corners_second[0], corners_first[1], corners_back),
    ]
    shape = green.shape[:2] + (NPAIR, green.shape[2], points // (2 * RING), 2 * points)
    return final(meta, offsets, parts, token, shape)


def solution(mesh):
    return jax.shard_map(
        per_device,
        mesh=mesh,
        in_specs=(P("gx", "gy", None, None, "sa", None), P()),
        out_specs=P("gx", "gy", None, None, "sa", None),
        check_vma=False,
    )
```

```python
import functools

import jax
import jax.numpy as jnp
from jax import lax
from jax.experimental import pallas as pl
from jax.experimental.pallas import tpu as pltpu
from jax.sharding import PartitionSpec as P

NPAIR = 4
RING = 4
LOOSE0, LOOSE1, DOWN, UP = range(4)
MIB = 1024 * 1024
EARLY = ((0, 0, UP), (0, 0, LOOSE0), (0, 0, LOOSE1), (0, 1, DOWN), (1, 0, LOOSE0))
FIRST = ((0, 2, DOWN), (0, 1, LOOSE0), (0, 1, LOOSE1), (0, 1, UP), (1, 1, LOOSE0))
LAST = ((1, 0, LOOSE1), (1, 0, DOWN), (1, 0, UP), (1, 1, LOOSE1), (1, 1, DOWN), (1, 1, UP))
OWN = ((0, 0), (0, 1), (1, 0), (1, 1))
BESIDE = ((2, 0), (2, 1))
ABOVE = ((0, 2), (1, 2))
CORNER_UP = ((2, 2),)
CORNER_DOWN = ((2, -1),)


def slot_table(offsets):
    dx = [offsets[k, 0] for k in range(NPAIR)]
    dy = [offsets[k, 1] for k in range(NPAIR)]
    code = [
        jnp.where(dx[k] == 0, dy[k], jnp.where(dy[k] == 0, 2, jnp.where(dy[k] < 0, 3, 4)))
        for k in range(NPAIR)
    ]
    rank = [
        sum((code[j] < code[k]).astype(jnp.int32) for j in range(NPAIR) if j != k) for k in range(NPAIR)
    ]

    def pick(values, slot):
        return sum(jnp.where(rank[k] == slot, values[k], 0) for k in range(NPAIR))

    return [(pick(dx, s), pick(dy, s), pick(list(range(NPAIR)), s)) for s in range(NPAIR)]


REMAINDER = 2.0**-8
REAL_STEPS = 128
IMAG_STEPS = 32
LADDER = (32, 16, 8, 4, 2, 1)


def encode(ref, index, value):
    points = value.shape[1] // 2
    high = value.astype(jnp.bfloat16)
    ref[index, :, : 2 * points] = high
    high = high.astype(jnp.float32)
    size = jnp.abs(high)
    inverse = jnp.where(size > 1e-37, 1.0 / jnp.maximum(size, 1e-37), 0.0)
    share = (value - high) * inverse
    real = jnp.floor(share[:, :points] * (REAL_STEPS / REMAINDER))
    real = jnp.clip(real, -REAL_STEPS, REAL_STEPS - 1)
    code = jnp.where(real >= 0, real + REAL_STEPS, real - (REAL_STEPS - 1))
    rest = jnp.floor(share[:, points:] * (IMAG_STEPS / REMAINDER)) + IMAG_STEPS
    rest = jnp.clip(rest, 0, 2 * IMAG_STEPS - 1)
    for k in LADDER:
        over = rest >= k
        code = jnp.where(over, code * 2.0**k, code)
        rest = jnp.where(over, rest - k, rest)
    ref[index, :, 2 * points :] = code.astype(jnp.bfloat16)


def decode(ref, index):
    points = ref.shape[2] // 3
    high = ref[index, :, : 2 * points].astype(jnp.float32)
    code = ref[index, :, 2 * points :].astype(jnp.float32)
    size = jnp.abs(code) * (1.0 / REAL_STEPS)
    imag = jnp.full_like(size, 0.5 - IMAG_STEPS)
    for k in LADDER:
        over = size >= 2.0**k
        size = jnp.where(over, size * 2.0**-k, size)
        imag = jnp.where(over, imag + k, imag)
    real = (size - 1.0) * REAL_STEPS + 0.5
    real = jnp.where(code >= 0, real, -real)
    share = jnp.concatenate([real * (REMAINDER / REAL_STEPS), imag * (REMAINDER / IMAG_STEPS)], axis=1)
    return high + share * jnp.abs(high)


def store_pieces(outs, place, meta, index, count):
    own_a, own_b, up_first, down_first, up_second, down_second = outs
    x_lo, y = meta[0], meta[1]
    half = place.shape[0] // 2
    rows = half // RING
    target = {
        (0, 0): (own_a, 0),
        (0, 1): (own_b, 0),
        (2, 0): (up_first, 0),
        (1, 1): (up_first, count),
        (2, 1): (down_first, 0),
        (3, 0): (down_first, count),
        (1, 0): (up_second, 0),
        (3, 1): (down_second, 0),
    }
    for (d, h), (ref, base) in target.items():
        start = lax.rem(x_lo + h, 2) * half + lax.rem(y + d, RING) * rows
        value = place[pl.ds(pl.multiple_of(start, rows), rows), :]
        if ref is up_first or ref is down_first:
            encode(ref, base + index, value)
        else:
            ref[base + index] = value


def load_tile(left, right, tile, own, parts):
    traces, points = parts[0].shape[-2:]
    for i, part in enumerate(parts):
        re, im = part[0], part[1]
        low = slice(2 * i * traces, (2 * i + 1) * traces)
        high = slice((2 * i + 1) * traces, (2 * i + 2) * traces)
        right[tile, low, :points] = re
        right[tile, high, :points] = im
        right[tile, low, points:] = im
        right[tile, high, points:] = -re
        if own is not None:
            left[own, :, low] = re.T
            left[own, :, high] = im.T


def early_kernel(meta, offsets, token, green, *refs):
    outs, (left, right, acc) = refs[:6], refs[7:]
    refs[6][...] = token[...]
    slots = slot_table(offsets)
    count = 2 * len(EARLY)
    for freq in range(2):
        for tx in range(2):
            for ty in range(2):
                load_tile(left, right, freq * 4 + tx * 2 + ty, freq * 4 + tx * 2 + ty, [green.at[tx, ty, freq]])
    for b, (tx, ty, slot) in enumerate(EARLY):
        dx, dy, _ = slots[slot]
        for freq in range(2):
            place = acc.at[freq]
            tile = freq * 4 + (tx + dx) * 2 + ty + dy
            place[...] = jnp.dot(left[freq * 4 + tx * 2 + ty], right[tile], preferred_element_type=jnp.float32)
            store_pieces(outs, place, meta, 2 * b + freq, count)


def late_kernel(groups, where, *refs):
    count = 3 + len(where)
    meta, offsets, token = refs[:3]
    outs, (out_token, left, right, acc) = refs[count:-4], refs[-4:]
    out_token[...] = token[...]
    sources = {}
    for ref, tiles in zip(refs[3:count], where):
        for i, tile in enumerate(tiles):
            sources.setdefault(tile, []).append(ref.at[i])
    for (tx, ty), parts in sources.items():
        load_tile(left, right, tx * 4 + ty + 1, tx * 3 + ty if tx < 2 else None, parts)
    slots = slot_table(offsets)
    step = 0
    for g, group in enumerate(groups):
        for b, (tx, ty, slot) in enumerate(group):
            dx, dy, _ = slots[slot]
            place = acc.at[step % 2]
            step += 1
            tile = (tx + dx) * 4 + ty + dy + 1
            place[...] = jnp.dot(left[tx * 3 + ty], right[tile], preferred_element_type=jnp.float32)
            store_pieces(outs[6 * g : 6 * g + 6], place, meta, b, len(group))


def call_blocks(kernel, counts, depth, tiles, lefts, points, arrays, token, name):
    meta, offsets, *values = arrays
    smem = pl.BlockSpec(memory_space=pltpu.SMEM)
    vmem = pl.BlockSpec(memory_space=pltpu.VMEM)
    rows = points // (2 * RING)
    out_shape = []
    for count in counts:
        kept = jax.ShapeDtypeStruct((count, rows, 2 * points), jnp.float32)
        sent = jax.ShapeDtypeStruct((2 * count, rows, 3 * points), jnp.bfloat16)
        out_shape += [kept, kept, sent, sent, kept, kept]
    *pieces, token = pl.pallas_call(
        kernel,
        out_shape=out_shape + [jax.ShapeDtypeStruct(token.shape, token.dtype)],
        in_specs=[smem, smem] + [vmem] * (1 + len(values)),
        out_specs=[vmem] * (len(out_shape) + 1),
        scratch_shapes=[
            pltpu.VMEM((lefts, points, depth), jnp.bfloat16),
            pltpu.VMEM((tiles, depth, 2 * points), jnp.bfloat16),
            pltpu.VMEM((2, points, 2 * points), jnp.float32),
        ],
        compiler_params=pltpu.CompilerParams(vmem_limit_bytes=(24 if len(values) > 1 else 14) * MIB),
        cost_estimate=pl.CostEstimate(flops=0, bytes_accessed=0, transcendentals=0),
        name=name,
    )(meta, offsets, token, *values)
    return [pieces[6 * g : 6 * g + 6] for g in range(len(counts))], token


def call_step(kernel, out_shape, token, arrays, name):
    vmem = pl.BlockSpec(memory_space=pltpu.VMEM)
    *outs, token = pl.pallas_call(
        kernel,
        out_shape=list(out_shape) + [jax.ShapeDtypeStruct(token.shape, token.dtype)],
        in_specs=[vmem] * (1 + len(arrays)),
        out_specs=[vmem] * (1 + len(out_shape)),
        compiler_params=pltpu.CompilerParams(vmem_limit_bytes=6 * MIB),
        cost_estimate=pl.CostEstimate(flops=0, bytes_accessed=0, transcendentals=0),
        name=name,
    )(token, *arrays)
    return outs, token


def swapped_kernel(token, mine, theirs, above_mine, above, beside, out_token):
    for i, part in enumerate((mine, theirs)):
        beside[i] = part[0]
    for tx in range(2):
        above[tx] = theirs[tx, 0]
    out_token[...] = token[...]


def corner_kernel(token, mine, theirs, up, down, out_token):
    for i, part in enumerate((mine, theirs)):
        up[i] = part[0, 0]
        down[i] = part[0, 1]
    out_token[...] = token[...]


def keep_kernel(token, own, before, after, rows, out_token):
    count = own.shape[0]
    for i in range(count):
        rows[i] = own[i] + decode(before, i) + decode(after, count + i)
    out_token[...] = token[...]


def give_kernel(token, kept, other, rows, out_token):
    rows[0] = kept[0]
    rows[1] = other[0]
    out_token[...] = token[...]


def second_kernel(token, up_received, down_received, up_own, down_own, *refs):
    up, down, out_token = refs[-3:]
    for i in range(up_own.shape[0]):
        encode(up, i, up_own[i] + decode(up_received, i))
        encode(down, i, down_own[i] + decode(down_received, i))
    out_token[...] = token[...]


def back_kernel(token, down_arrived, own, up_received, *refs):
    out, out_token = refs[-2:]
    count = own.shape[0]
    for i in range(count):
        out[i] = own[i] + decode(up_received, count + i) + decode(down_arrived, i)
    out_token[...] = token[...]


def final_kernel(meta, offsets, *refs):
    given, _, out = refs[-3:]
    x_lo = meta[0]
    slots = slot_table(offsets)
    for g, group in enumerate((EARLY, FIRST, LAST)):
        kept, other = refs[2 * g : 2 * g + 2]
        for b, (tx, ty, slot) in enumerate(group):
            pair = slots[slot][2]
            if g == 0:
                for freq in range(2):
                    out[tx, ty, pair, freq] = kept[2 * b + freq] + other[2 * b + freq]
            elif ty == 2:
                out[tx, 0, pair, x_lo] = given[0]
                out[tx, 0, pair, 1 - x_lo] = given[1]
            else:
                out[tx, ty, pair, x_lo] = kept[b]
                out[tx, ty, pair, 1 - x_lo] = other[b]


def final(meta, offsets, parts, given, token, shape):
    smem = pl.BlockSpec(memory_space=pltpu.SMEM)
    vmem = pl.BlockSpec(memory_space=pltpu.VMEM)
    flat = [part for group in parts for part in group]
    return pl.pallas_call(
        final_kernel,
        out_shape=jax.ShapeDtypeStruct(shape, jnp.float32),
        in_specs=[smem, smem] + [vmem] * (len(flat) + 2),
        out_specs=vmem,
        compiler_params=pltpu.CompilerParams(vmem_limit_bytes=10 * MIB),
        cost_estimate=pl.CostEstimate(flops=0, bytes_accessed=0, transcendentals=0),
        name="place_blocks",
    )(meta, offsets, *flat, given, token)


def per_device(green, offsets):
    points, traces = green.shape[5], green.shape[4]
    gx, gy = lax.axis_size("gx"), lax.axis_size("gy")
    sa = lax.axis_index("sa")
    x_lo, y = sa // RING, sa % RING
    meta = jnp.stack([x_lo, y]).astype(jnp.int32)

    def swap(value):
        return lax.ppermute(value, "sa", [(i, (i + RING) % (2 * RING)) for i in range(2 * RING)])

    def around(value, steps):
        return lax.ppermute(value, "sa", [(h * RING + i, h * RING + (i + steps) % RING) for h in range(2) for i in range(RING)])

    def tiles_from(value, dx, dy):
        perm = [
            ((ix + dx) * gy + iy + dy, ix * gy + iy)
            for ix in range(gx - dx)
            for iy in range(max(0, -dy), min(gy, gy - dy))
        ]
        return lax.ppermute(value, ("gx", "gy"), perm)

    def first(pieces):
        return around(pieces[2], 1), around(pieces[3], -1)

    def second(pieces, received, token, also=()):
        up, down = pieces[4], pieces[5]
        count, rows, columns = up.shape
        sent = jax.ShapeDtypeStruct((count, rows, columns // 2 * 3), jnp.bfloat16)
        (up, down), token = call_step(second_kernel, [sent, sent], token, [*received, up, down, *also], "second")
        return (around(up, 1), around(down, -1)), token

    def back(pieces, received, arrived, token):
        own = pieces[1]
        (out,), token = call_step(back_kernel, [own], token, [arrived[1], own, received[0], arrived[0]], "back")
        return swap(out), token

    def keep(pieces, received, arrived, token):
        (rows,), token = call_step(keep_kernel, [pieces[0]], token, [pieces[0], arrived[0], received[1]], "keep")
        return rows, token

    def blocks(group, inputs, token, name):
        kernel = functools.partial(late_kernel, (group,), [where for where, _ in inputs])
        arrays = [meta, offsets] + [value for _, value in inputs]
        (pieces,), token = call_blocks(kernel, [len(group)], 4 * traces, 12, 6, points, arrays, token, name)
        return pieces, token

    token = jnp.zeros((8, 128), jnp.float32)
    theirs = swap(lax.dynamic_index_in_dim(green, 1 - x_lo, 2, keepdims=False))
    mine = lax.dynamic_index_in_dim(green, x_lo, 2, keepdims=False)
    above_mine = tiles_from(mine[:, 0], 0, 1)
    early_count = 2 * len(EARLY)
    (early,), token = call_blocks(
        early_kernel, [early_count], 2 * traces, 8, 8, points, [meta, offsets, green], token, "early_blocks"
    )
    early_first = first(early)
    dtype, shape = green.dtype, mine.shape[2:]
    pair = jax.ShapeDtypeStruct((2,) + shape, dtype)
    pairs = jax.ShapeDtypeStruct((2, 2) + shape, dtype)
    (above, beside), token = call_step(swapped_kernel, [pair, pairs], token, [mine, theirs, above_mine], "swapped")
    above_theirs = tiles_from(above, 0, 1)
    beside = tiles_from(beside, 1, 0)
    early_second, token = second(early, early_first, token)
    (corner_up, corner_down), token = call_step(corner_kernel, [pair, pair], token, [mine, theirs], "corner")
    corner_up = tiles_from(corner_up, 1, 1)
    corner_down = tiles_from(corner_down, 1, -1)
    tiles = [(OWN, mine.reshape(4, *shape)), (OWN, theirs.reshape(4, *shape)), (ABOVE, above_mine), (ABOVE, above_theirs)]
    one, token = blocks(FIRST, tiles, token, "first_blocks")
    one_first = first(one)
    early_back, token = back(early, early_first, early_second, token)
    early_kept, token = keep(early, early_first, early_second, token)
    tiles += [(BESIDE, beside[0]), (BESIDE, beside[1]), (CORNER_UP, corner_up[:1]), (CORNER_UP, corner_up[1:])]
    tiles += [(CORNER_DOWN, corner_down[:1]), (CORNER_DOWN, corner_down[1:])]
    two, token = blocks(LAST, tiles, token, "last_blocks")
    two_first = first(two)
    one_second, token = second(one, one_first, token, [early_back])
    two_second, token = second(two, two_first, token)
    one_back, token = back(one, one_first, one_second, token)
    one_kept, token = keep(one, one_first, one_second, token)
    rows = jax.ShapeDtypeStruct((2,) + one_kept.shape[1:], jnp.float32)
    (given,), token = call_step(give_kernel, [rows], token, [one_kept, one_back], "give")
    given = tiles_from(given, 0, -1)
    two_back, token = back(two, two_first, two_second, token)
    two_kept, token = keep(two, two_first, two_second, token)
    parts = [(early_kept, early_back), (one_kept, one_back), (two_kept, two_back)]
    shape = green.shape[:2] + (NPAIR, green.shape[2], points // (2 * RING), 2 * points)
    return final(meta, offsets, parts, given, token, shape)


def solution(mesh):
    return jax.shard_map(
        per_device,
        mesh=mesh,
        in_specs=(P("gx", "gy", None, None, "sa", None), P()),
        out_specs=P("gx", "gy", None, None, "sa", None),
        check_vma=False,
    )
```

```python
import functools

import jax
import jax.numpy as jnp
from jax import lax
from jax.experimental import pallas as pl
from jax.experimental.pallas import tpu as pltpu
from jax.sharding import PartitionSpec as P

NPAIR = 4
RING = 4
LOOSE0, LOOSE1, DOWN, UP = range(4)
MIB = 1024 * 1024
EARLY = ((0, 0, UP), (0, 0, LOOSE0), (0, 0, LOOSE1), (0, 1, DOWN), (1, 0, LOOSE0))
GIVEN = 2
FIRST = ((0, 2, DOWN), (1, 2, DOWN), (0, 1, LOOSE0), (0, 1, LOOSE1), (0, 1, UP), (1, 1, LOOSE0))
LAST = ((1, 0, LOOSE1), (1, 0, UP), (1, 1, LOOSE1), (1, 1, DOWN), (1, 1, UP))
OWN = ((0, 0), (0, 1), (1, 0), (1, 1))
BESIDE = ((2, 0), (2, 1))
ABOVE = ((0, 2), (1, 2))
CORNER = ((2, 2),)


def slot_table(offsets):
    dx = [offsets[k, 0] for k in range(NPAIR)]
    dy = [offsets[k, 1] for k in range(NPAIR)]
    code = [
        jnp.where(dx[k] == 0, dy[k], jnp.where(dy[k] == 0, 2, jnp.where(dy[k] < 0, 3, 4)))
        for k in range(NPAIR)
    ]
    rank = [
        sum((code[j] < code[k]).astype(jnp.int32) for j in range(NPAIR) if j != k) for k in range(NPAIR)
    ]

    def pick(values, slot):
        return sum(jnp.where(rank[k] == slot, values[k], 0) for k in range(NPAIR))

    return [(pick(dx, s), pick(dy, s), pick(list(range(NPAIR)), s)) for s in range(NPAIR)]


REMAINDER = 2.0**-8
REAL_STEPS = 127
IMAG_STEPS = 31


def encode(ref, index, value):
    points = value.shape[1] // 2
    high = value.astype(jnp.bfloat16)
    ref[index, :, : 2 * points] = high
    high = high.astype(jnp.float32)
    size = jnp.abs(high)
    inverse = jnp.where(size > 1e-37, 1.0 / jnp.maximum(size, 1e-37), 0.0)
    share = (value - high) * inverse
    real = jnp.floor(share[:, :points] * (REAL_STEPS / REMAINDER) + 0.5)
    real = jnp.clip(real, -REAL_STEPS, REAL_STEPS)
    code = jnp.where(real >= 0, real + 128, real - 127)
    rest = jnp.floor(share[:, points:] * (IMAG_STEPS / REMAINDER) + 0.5)
    rest = jnp.clip(rest, -IMAG_STEPS, IMAG_STEPS) + IMAG_STEPS
    ref[index, :, 2 * points :] = (code * jnp.exp2(rest)).astype(jnp.bfloat16)


def decode(ref, index):
    points = ref.shape[2] // 3
    high = ref[index, :, : 2 * points].astype(jnp.float32)
    code = ref[index, :, 2 * points :].astype(jnp.float32)
    size = jnp.maximum(jnp.abs(code) * (1.0 / 128), 1.0)
    power = jnp.floor(jnp.log2(size) + 0.002)
    imag = power - IMAG_STEPS
    real = size * jnp.exp2(-power) * 128 - 128
    real = jnp.where(code >= 0, real, -1 - real)
    share = jnp.concatenate([real * (REMAINDER / REAL_STEPS), imag * (REMAINDER / IMAG_STEPS)], axis=1)
    return high + share * jnp.abs(high)


def store_pieces(outs, place, meta, index, count):
    own_a, own_b, up_first, down_first, up_second, down_second = outs
    x_lo, y = meta[0], meta[1]
    half = place.shape[0] // 2
    rows = half // RING
    target = {
        (0, 0): (own_a, 0),
        (0, 1): (own_b, 0),
        (2, 0): (up_first, 0),
        (1, 1): (up_first, count),
        (2, 1): (down_first, 0),
        (3, 0): (down_first, count),
        (1, 0): (up_second, 0),
        (3, 1): (down_second, 0),
    }
    for (d, h), (ref, base) in target.items():
        start = lax.rem(x_lo + h, 2) * half + lax.rem(y + d, RING) * rows
        value = place[pl.ds(pl.multiple_of(start, rows), rows), :]
        if ref is up_first or ref is down_first:
            encode(ref, base + index, value)
        else:
            ref[base + index] = value


def load_tile(left, right, tile, own, parts):
    traces, points = parts[0].shape[-2:]
    for i, part in enumerate(parts):
        re, im = part[0], part[1]
        low = slice(2 * i * traces, (2 * i + 1) * traces)
        high = slice((2 * i + 1) * traces, (2 * i + 2) * traces)
        right[tile, low, :points] = re
        right[tile, high, :points] = im
        right[tile, low, points:] = im
        right[tile, high, points:] = -re
        if own is not None:
            left[own, :, low] = re.T
            left[own, :, high] = im.T


def early_kernel(meta, offsets, token, green, *refs):
    outs, (left, right, acc) = refs[:6], refs[7:]
    refs[6][...] = token[...]
    slots = slot_table(offsets)
    count = 2 * len(EARLY)
    for freq in range(2):
        for tx in range(2):
            for ty in range(2):
                load_tile(left, right, freq * 4 + tx * 2 + ty, freq * 4 + tx * 2 + ty, [green.at[tx, ty, freq]])
    for b, (tx, ty, slot) in enumerate(EARLY):
        dx, dy, _ = slots[slot]
        for freq in range(2):
            place = acc.at[freq]
            tile = freq * 4 + (tx + dx) * 2 + ty + dy
            place[...] = jnp.dot(left[freq * 4 + tx * 2 + ty], right[tile], preferred_element_type=jnp.float32)
            store_pieces(outs, place, meta, 2 * b + freq, count)


def late_kernel(groups, where, *refs):
    count = 3 + len(where)
    meta, offsets, token = refs[:3]
    outs, (out_token, left, right, acc) = refs[count:-4], refs[-4:]
    out_token[...] = token[...]
    sources = {}
    for ref, tiles in zip(refs[3:count], where):
        for i, tile in enumerate(tiles):
            sources.setdefault(tile, []).append(ref.at[i])
    for (tx, ty), parts in sources.items():
        load_tile(left, right, tx * 3 + ty, tx * 3 + ty if tx < 2 else None, parts)
    slots = slot_table(offsets)
    step = 0
    for g, group in enumerate(groups):
        for b, (tx, ty, slot) in enumerate(group):
            dx, dy, _ = slots[slot]
            place = acc.at[step % 2]
            step += 1
            tile = (tx + dx) * 3 + ty + dy
            place[...] = jnp.dot(left[tx * 3 + ty], right[tile], preferred_element_type=jnp.float32)
            store_pieces(outs[6 * g : 6 * g + 6], place, meta, b, len(group))


def call_blocks(kernel, counts, depth, tiles, lefts, points, arrays, token, name):
    meta, offsets, *values = arrays
    smem = pl.BlockSpec(memory_space=pltpu.SMEM)
    vmem = pl.BlockSpec(memory_space=pltpu.VMEM)
    rows = points // (2 * RING)
    out_shape = []
    for count in counts:
        kept = jax.ShapeDtypeStruct((count, rows, 2 * points), jnp.float32)
        sent = jax.ShapeDtypeStruct((2 * count, rows, 3 * points), jnp.bfloat16)
        out_shape += [kept, kept, sent, sent, kept, kept]
    *pieces, token = pl.pallas_call(
        kernel,
        out_shape=out_shape + [jax.ShapeDtypeStruct(token.shape, token.dtype)],
        in_specs=[smem, smem] + [vmem] * (1 + len(values)),
        out_specs=[vmem] * (len(out_shape) + 1),
        scratch_shapes=[
            pltpu.VMEM((lefts, points, depth), jnp.bfloat16),
            pltpu.VMEM((tiles, depth, 2 * points), jnp.bfloat16),
            pltpu.VMEM((2, points, 2 * points), jnp.float32),
        ],
        compiler_params=pltpu.CompilerParams(vmem_limit_bytes=(24 if len(values) > 1 else 14) * MIB),
        cost_estimate=pl.CostEstimate(flops=0, bytes_accessed=0, transcendentals=0),
        name=name,
    )(meta, offsets, token, *values)
    return [pieces[6 * g : 6 * g + 6] for g in range(len(counts))], token


def call_step(kernel, out_shape, token, arrays, name, size=0):
    vmem = pl.BlockSpec(memory_space=pltpu.VMEM)
    *outs, token = pl.pallas_call(
        kernel,
        out_shape=list(out_shape) + [jax.ShapeDtypeStruct(token.shape, token.dtype)],
        in_specs=[vmem] * (1 + len(arrays)),
        out_specs=[vmem] * (1 + len(out_shape)),
        compiler_params=pltpu.CompilerParams(vmem_limit_bytes=6 * MIB),
        cost_estimate=pl.CostEstimate(flops=0, bytes_accessed=size, transcendentals=0),
        name=name,
    )(token, *arrays)
    return outs, token


def swapped_kernel(token, mine, theirs, above_mine, above, beside, corner, out_token):
    for i, part in enumerate((mine, theirs)):
        beside[i] = part[0]
        corner[i] = part[0, 0]
    for tx in range(2):
        above[tx] = theirs[tx, 0]
    out_token[...] = token[...]


def keep_kernel(token, own, before, after, rows, out_token):
    count = own.shape[0]
    for i in range(count):
        rows[i] = own[i] + decode(before, i) + decode(after, count + i)
    out_token[...] = token[...]


def give_kernel(token, kept, other, rows, out_token):
    for i in range(GIVEN):
        encode(rows, i, kept[i])
        rows[GIVEN + i] = other[i]
    out_token[...] = token[...]


def second_kernel(token, up_received, down_received, up_own, down_own, *refs):
    up, down, out_token = refs[-3:]
    for i in range(up_own.shape[0]):
        encode(up, i, up_own[i] + decode(up_received, i))
        encode(down, i, down_own[i] + decode(down_received, i))
    for i in range(up_own.shape[0], up.shape[0]):
        up[i] = jnp.zeros_like(up[i])
        down[i] = jnp.zeros_like(down[i])
    out_token[...] = token[...]


def back_kernel(token, down_arrived, own, up_received, *refs):
    out, out_token = refs[-2:]
    count = own.shape[0]
    for i in range(count):
        encode(out, i, own[i] + decode(up_received, count + i) + decode(down_arrived, i))
    out_token[...] = token[...]


def final_kernel(meta, offsets, *refs):
    given, _, out = refs[-3:]
    x_lo = meta[0]
    slots = slot_table(offsets)
    for g, group in enumerate((EARLY, FIRST, LAST)):
        kept, other = refs[2 * g : 2 * g + 2]
        for b, (tx, ty, slot) in enumerate(group):
            pair = slots[slot][2]
            if g == 0:
                for freq in range(2):
                    out[tx, ty, pair, freq] = kept[2 * b + freq] + decode(other, 2 * b + freq)
            elif ty == 2:
                out[tx, 0, pair, x_lo] = decode(given, b)
                out[tx, 0, pair, 1 - x_lo] = decode(given, GIVEN + b)
            else:
                out[tx, ty, pair, x_lo] = kept[b]
                out[tx, ty, pair, 1 - x_lo] = decode(other, b)


def final(meta, offsets, parts, given, token, shape):
    smem = pl.BlockSpec(memory_space=pltpu.SMEM)
    vmem = pl.BlockSpec(memory_space=pltpu.VMEM)
    flat = [part for group in parts for part in group]
    return pl.pallas_call(
        final_kernel,
        out_shape=jax.ShapeDtypeStruct(shape, jnp.float32),
        in_specs=[smem, smem] + [vmem] * (len(flat) + 2),
        out_specs=vmem,
        compiler_params=pltpu.CompilerParams(vmem_limit_bytes=10 * MIB),
        cost_estimate=pl.CostEstimate(flops=0, bytes_accessed=0, transcendentals=0),
        name="place_blocks",
    )(meta, offsets, *flat, given, token)


def per_device(green, offsets):
    points, traces = green.shape[5], green.shape[4]
    gx, gy = lax.axis_size("gx"), lax.axis_size("gy")
    sa = lax.axis_index("sa")
    x_lo, y = sa // RING, sa % RING
    meta = jnp.stack([x_lo, y]).astype(jnp.int32)

    def swap(value):
        return lax.ppermute(value, "sa", [(i, (i + RING) % (2 * RING)) for i in range(2 * RING)])

    def around(value, steps):
        return lax.ppermute(value, "sa", [(h * RING + i, h * RING + (i + steps) % RING) for h in range(2) for i in range(RING)])

    def tiles_from(value, dx, dy):
        perm = [
            ((ix + dx) * gy + iy + dy, ix * gy + iy)
            for ix in range(gx - dx)
            for iy in range(max(0, -dy), min(gy, gy - dy))
        ]
        return lax.ppermute(value, ("gx", "gy"), perm)

    def coded(value, spare=0):
        count, rows, columns = value.shape
        return jax.ShapeDtypeStruct((count + spare, rows, columns // 2 * 3), jnp.bfloat16)

    def first(pieces):
        return around(pieces[2], 1), around(pieces[3], -1)

    def second(pieces, received, token, also=(), spare=0):
        up, down = pieces[4], pieces[5]
        (up, down), token = call_step(second_kernel, [coded(up, spare), coded(down, spare)], token, [*received, up, down, *also], "second")
        return (around(up, 1), around(down, -1)), token

    def back(pieces, received, arrived, token):
        own = pieces[1]
        (out,), token = call_step(back_kernel, [coded(own)], token, [arrived[1], own, received[0], arrived[0]], "back")
        return swap(out), token

    def keep(pieces, received, arrived, token):
        (rows,), token = call_step(keep_kernel, [pieces[0]], token, [pieces[0], arrived[0], received[1]], "keep", 16 * MIB)
        return rows, token

    def blocks(groups, inputs, token, name):
        kernel = functools.partial(late_kernel, groups, [where for where, _ in inputs])
        arrays = [meta, offsets] + [value for _, value in inputs]
        return call_blocks(kernel, [len(group) for group in groups], 4 * traces, 9, 6, points, arrays, token, name)

    token = jnp.zeros((8, 128), jnp.float32)
    theirs = swap(lax.dynamic_index_in_dim(green, 1 - x_lo, 2, keepdims=False))
    mine = lax.dynamic_index_in_dim(green, x_lo, 2, keepdims=False)
    above_mine = tiles_from(mine[:, 0], 0, 1)
    early_count = 2 * len(EARLY)
    (early,), token = call_blocks(
        early_kernel, [early_count], 2 * traces, 8, 8, points, [meta, offsets, green], token, "early_blocks"
    )
    early_first = first(early)
    dtype, shape = green.dtype, mine.shape[2:]
    pair = jax.ShapeDtypeStruct((2,) + shape, dtype)
    pairs = jax.ShapeDtypeStruct((2, 2) + shape, dtype)
    sent, token = call_step(swapped_kernel, [pair, pairs, pair], token, [mine, theirs, above_mine], "swapped")
    above, beside, corner = sent
    above_theirs = tiles_from(above, 0, 1)
    beside = tiles_from(beside, 1, 0)
    corner = tiles_from(corner, 1, 1)
    early_second, token = second(early, early_first, token)
    tiles = [(OWN, mine.reshape(4, *shape)), (OWN, theirs.reshape(4, *shape)), (ABOVE, above_mine), (ABOVE, above_theirs)]
    tiles += [(BESIDE, beside[0]), (BESIDE, beside[1])]
    (one,), token = blocks((FIRST,), tiles, token, "first_blocks")
    one_first = first(one)
    early_back, token = back(early, early_first, early_second, token)
    tiles += [(CORNER, corner[:1]), (CORNER, corner[1:])]
    (two,), token = blocks((LAST,), tiles, token, "last_blocks")
    two_first = first(two)
    one_second, token = second(one, one_first, token, [early_back])
    two_second, token = second(two, two_first, token)
    one_back, token = back(one, one_first, one_second, token)
    two_back, token = back(two, two_first, two_second, token)
    one_kept, token = keep(one, one_first, one_second, token)
    rows = jax.ShapeDtypeStruct((2 * GIVEN,) + one_back.shape[1:], one_back.dtype)
    (given,), token = call_step(give_kernel, [rows], token, [one_kept, one_back], "give")
    given = tiles_from(given, 0, -1)
    early_kept, token = keep(early, early_first, early_second, token)
    two_kept, token = keep(two, two_first, two_second, token)
    parts = [(early_kept, early_back), (one_kept, one_back), (two_kept, two_back)]
    shape = green.shape[:2] + (NPAIR, green.shape[2], points // (2 * RING), 2 * points)
    return final(meta, offsets, parts, given, token, shape)


def solution(mesh):
    return jax.shard_map(
        per_device,
        mesh=mesh,
        in_specs=(P("gx", "gy", None, None, "sa", None), P()),
        out_specs=P("gx", "gy", None, None, "sa", None),
        check_vma=False,
    )
```

```python
import functools

import jax
import jax.numpy as jnp
from jax import lax
from jax.experimental import pallas as pl
from jax.experimental.pallas import tpu as pltpu
from jax.sharding import PartitionSpec as P

NPAIR = 4
RING = 4
LOOSE0, LOOSE1, DOWN, UP = range(4)
MIB = 1024 * 1024
EARLY = ((0, 0, UP), (0, 0, LOOSE0), (0, 0, LOOSE1), (0, 1, DOWN), (1, 0, LOOSE0))
GIVEN = 2
FIRST = ((0, 2, DOWN), (1, 2, DOWN), (0, 1, LOOSE0), (0, 1, LOOSE1), (0, 1, UP), (1, 1, LOOSE0))
LAST = ((1, 0, LOOSE1), (1, 0, UP), (1, 1, LOOSE1), (1, 1, DOWN), (1, 1, UP))

WAITING = 100_000_000_000
OWN = ((0, 0), (0, 1), (1, 0), (1, 1))
BESIDE = ((2, 0), (2, 1))
ABOVE = ((0, 2), (1, 2))
CORNER = ((2, 2),)


def slot_table(offsets):
    dx = [offsets[k, 0] for k in range(NPAIR)]
    dy = [offsets[k, 1] for k in range(NPAIR)]
    code = [
        jnp.where(dx[k] == 0, dy[k], jnp.where(dy[k] == 0, 2, jnp.where(dy[k] < 0, 3, 4)))
        for k in range(NPAIR)
    ]
    rank = [
        sum((code[j] < code[k]).astype(jnp.int32) for j in range(NPAIR) if j != k) for k in range(NPAIR)
    ]

    def pick(values, slot):
        return sum(jnp.where(rank[k] == slot, values[k], 0) for k in range(NPAIR))

    return [(pick(dx, s), pick(dy, s), pick(list(range(NPAIR)), s)) for s in range(NPAIR)]


REMAINDER = 2.0**-8
REAL_STEPS = 127
IMAG_STEPS = 31


def encode(ref, index, value):
    points = value.shape[1] // 2
    high = value.astype(jnp.bfloat16)
    ref[index, :, : 2 * points] = high
    high = high.astype(jnp.float32)
    size = jnp.abs(high)
    inverse = jnp.where(size > 1e-37, 1.0 / jnp.maximum(size, 1e-37), 0.0)
    share = (value - high) * inverse
    real = jnp.floor(share[:, :points] * (REAL_STEPS / REMAINDER) + 0.5)
    real = jnp.clip(real, -REAL_STEPS, REAL_STEPS)
    code = jnp.where(real >= 0, real + 128, real - 127)
    rest = jnp.floor(share[:, points:] * (IMAG_STEPS / REMAINDER) + 0.5)
    rest = jnp.clip(rest, -IMAG_STEPS, IMAG_STEPS) + IMAG_STEPS
    ref[index, :, 2 * points :] = (code * jnp.exp2(rest)).astype(jnp.bfloat16)


def decode(ref, index):
    points = ref.shape[2] // 3
    high = ref[index, :, : 2 * points].astype(jnp.float32)
    code = ref[index, :, 2 * points :].astype(jnp.float32)
    size = jnp.maximum(jnp.abs(code) * (1.0 / 128), 1.0)
    power = jnp.floor(jnp.log2(size) + 0.002)
    imag = power - IMAG_STEPS
    real = size * jnp.exp2(-power) * 128 - 128
    real = jnp.where(code >= 0, real, -1 - real)
    share = jnp.concatenate([real * (REMAINDER / REAL_STEPS), imag * (REMAINDER / IMAG_STEPS)], axis=1)
    return high + share * jnp.abs(high)


def store_pieces(outs, place, meta, index, count):
    own_a, own_b, up_first, down_first, up_second, down_second = outs
    x_lo, y = meta[0], meta[1]
    half = place.shape[0] // 2
    rows = half // RING
    target = {
        (0, 0): (own_a, 0),
        (0, 1): (own_b, 0),
        (2, 0): (up_first, 0),
        (1, 1): (up_first, count),
        (2, 1): (down_first, 0),
        (3, 0): (down_first, count),
        (1, 0): (up_second, 0),
        (3, 1): (down_second, 0),
    }
    for (d, h), (ref, base) in target.items():
        start = lax.rem(x_lo + h, 2) * half + lax.rem(y + d, RING) * rows
        value = place[pl.ds(pl.multiple_of(start, rows), rows), :]
        if ref is up_first or ref is down_first:
            encode(ref, base + index, value)
        else:
            ref[base + index] = value


def load_tile(left, right, tile, own, parts):
    traces, points = parts[0].shape[-2:]
    for i, part in enumerate(parts):
        re, im = part[0], part[1]
        low = slice(2 * i * traces, (2 * i + 1) * traces)
        high = slice((2 * i + 1) * traces, (2 * i + 2) * traces)
        right[tile, low, :points] = re
        right[tile, high, :points] = im
        right[tile, low, points:] = im
        right[tile, high, points:] = -re
        if own is not None:
            left[own, :, low] = re.T
            left[own, :, high] = im.T


def early_kernel(meta, offsets, token, green, *refs):
    outs, (left, right, acc) = refs[:6], refs[7:]
    refs[6][...] = token[...]
    slots = slot_table(offsets)
    count = 2 * len(EARLY)
    for freq in range(2):
        for tx in range(2):
            for ty in range(2):
                load_tile(left, right, freq * 4 + tx * 2 + ty, freq * 4 + tx * 2 + ty, [green.at[tx, ty, freq]])
    for b, (tx, ty, slot) in enumerate(EARLY):
        dx, dy, _ = slots[slot]
        for freq in range(2):
            place = acc.at[freq]
            tile = freq * 4 + (tx + dx) * 2 + ty + dy
            place[...] = jnp.dot(left[freq * 4 + tx * 2 + ty], right[tile], preferred_element_type=jnp.float32)
            store_pieces(outs, place, meta, 2 * b + freq, count)


def late_kernel(groups, where, *refs):
    count = 3 + len(where)
    meta, offsets, token = refs[:3]
    outs, (out_token, left, right, acc) = refs[count:-4], refs[-4:]
    out_token[...] = token[...]
    sources = {}
    for ref, tiles in zip(refs[3:count], where):
        for i, tile in enumerate(tiles):
            sources.setdefault(tile, []).append(ref.at[i])
    for (tx, ty), parts in sources.items():
        load_tile(left, right, tx * 3 + ty, tx * 3 + ty if tx < 2 else None, parts)
    slots = slot_table(offsets)
    step = 0
    for g, group in enumerate(groups):
        for b, (tx, ty, slot) in enumerate(group):
            dx, dy, _ = slots[slot]
            place = acc.at[step % 2]
            step += 1
            tile = (tx + dx) * 3 + ty + dy
            place[...] = jnp.dot(left[tx * 3 + ty], right[tile], preferred_element_type=jnp.float32)
            store_pieces(outs[6 * g : 6 * g + 6], place, meta, b, len(group))


def call_blocks(kernel, counts, depth, tiles, lefts, points, arrays, token, name):
    meta, offsets, *values = arrays
    smem = pl.BlockSpec(memory_space=pltpu.SMEM)
    vmem = pl.BlockSpec(memory_space=pltpu.VMEM)
    rows = points // (2 * RING)
    out_shape = []
    for count in counts:
        kept = jax.ShapeDtypeStruct((count, rows, 2 * points), jnp.float32)
        sent = jax.ShapeDtypeStruct((2 * count, rows, 3 * points), jnp.bfloat16)
        out_shape += [kept, kept, sent, sent, kept, kept]
    *pieces, token = pl.pallas_call(
        kernel,
        out_shape=out_shape + [jax.ShapeDtypeStruct(token.shape, token.dtype)],
        in_specs=[smem, smem] + [vmem] * (1 + len(values)),
        out_specs=[vmem] * (len(out_shape) + 1),
        scratch_shapes=[
            pltpu.VMEM((lefts, points, depth), jnp.bfloat16),
            pltpu.VMEM((tiles, depth, 2 * points), jnp.bfloat16),
            pltpu.VMEM((2, points, 2 * points), jnp.float32),
        ],
        compiler_params=pltpu.CompilerParams(vmem_limit_bytes=(24 if len(values) > 1 else 14) * MIB),
        cost_estimate=pl.CostEstimate(flops=0, bytes_accessed=0, transcendentals=0),
        name=name,
    )(meta, offsets, token, *values)
    return [pieces[6 * g : 6 * g + 6] for g in range(len(counts))], token


def call_step(kernel, out_shape, token, arrays, name, size=0):
    vmem = pl.BlockSpec(memory_space=pltpu.VMEM)
    *outs, token = pl.pallas_call(
        kernel,
        out_shape=list(out_shape) + [jax.ShapeDtypeStruct(token.shape, token.dtype)],
        in_specs=[vmem] * (1 + len(arrays)),
        out_specs=[vmem] * (1 + len(out_shape)),
        compiler_params=pltpu.CompilerParams(vmem_limit_bytes=6 * MIB),
        cost_estimate=pl.CostEstimate(flops=size, bytes_accessed=0, transcendentals=0),
        name=name,
    )(token, *arrays)
    return outs, token


def swapped_kernel(token, mine, theirs, above_mine, above, beside, corner, out_token):
    for i, part in enumerate((mine, theirs)):
        beside[i] = part[0]
        corner[i] = part[0, 0]
    for tx in range(2):
        above[tx] = theirs[tx, 0]
    out_token[...] = token[...]


def keep_kernel(token, own, before, after, *refs):
    rows, out_token = refs[-2:]
    count = own.shape[0]
    for i in range(count):
        value = own[i] + decode(before, i) + decode(after, count + i)
        for other in refs[:-2]:
            value = value + decode(other, i)
        rows[i] = value
    out_token[...] = token[...]


def give_kernel(token, kept, other, rows, out_token):
    for i in range(GIVEN):
        encode(rows, i, kept[i])
        rows[GIVEN + i] = other[i]
    out_token[...] = token[...]


def read_kernel(token, sums, rows, out_token):
    for i in range(sums.shape[0]):
        rows[i] = decode(sums, i)
    out_token[...] = token[...]


def second_kernel(token, up_received, down_received, up_own, down_own, *refs):
    up, down, out_token = refs[-3:]
    for i in range(up_own.shape[0]):
        encode(up, i, up_own[i] + decode(up_received, i))
        encode(down, i, down_own[i] + decode(down_received, i))
    out_token[...] = token[...]


def back_kernel(token, down_arrived, own, up_received, *refs):
    outs, out_token = refs[1:-1], refs[-1]
    count = own.shape[0]
    for i in range(count):
        value = own[i] + decode(up_received, count + i) + decode(down_arrived, i)
        first = outs[0].shape[0]
        encode(outs[0] if i < first else outs[1], i if i < first else i - first, value)
    out_token[...] = token[...]


def final_kernel(meta, offsets, early, kept_one, kept_two, other_one, other_two, given, token, out):
    x_lo = meta[0]
    slots = slot_table(offsets)
    for b, (tx, ty, slot) in enumerate(EARLY):
        for freq in range(2):
            out[tx, ty, slots[slot][2], freq] = early[2 * b + freq]
    for b, (tx, ty, slot) in enumerate(FIRST + LAST):
        pair = slots[slot][2]
        if b < GIVEN:
            out[tx, 0, pair, x_lo] = decode(given, b)
            out[tx, 0, pair, 1 - x_lo] = decode(given, GIVEN + b)
        else:
            late = b >= len(FIRST)
            out[tx, ty, pair, x_lo] = kept_two[b - len(FIRST)] if late else kept_one[b]
            out[tx, ty, pair, 1 - x_lo] = other_two[b - len(FIRST)] if late else other_one[b - GIVEN]


def final(meta, offsets, parts, token, shape):
    smem = pl.BlockSpec(memory_space=pltpu.SMEM)
    vmem = pl.BlockSpec(memory_space=pltpu.VMEM)
    return pl.pallas_call(
        final_kernel,
        out_shape=jax.ShapeDtypeStruct(shape, jnp.float32),
        in_specs=[smem, smem] + [vmem] * (len(parts) + 1),
        out_specs=vmem,
        compiler_params=pltpu.CompilerParams(vmem_limit_bytes=10 * MIB),
        cost_estimate=pl.CostEstimate(flops=0, bytes_accessed=0, transcendentals=0),
        name="place_blocks",
    )(meta, offsets, *parts, token)


def per_device(green, offsets):
    points, traces = green.shape[5], green.shape[4]
    gx, gy = lax.axis_size("gx"), lax.axis_size("gy")
    sa = lax.axis_index("sa")
    x_lo, y = sa // RING, sa % RING
    meta = jnp.stack([x_lo, y]).astype(jnp.int32)

    def swap(value):
        return lax.ppermute(value, "sa", [(i, (i + RING) % (2 * RING)) for i in range(2 * RING)])

    def around(value, steps):
        return lax.ppermute(value, "sa", [(h * RING + i, h * RING + (i + steps) % RING) for h in range(2) for i in range(RING)])

    def tiles_from(value, dx, dy):
        perm = [
            ((ix + dx) * gy + iy + dy, ix * gy + iy)
            for ix in range(gx - dx)
            for iy in range(max(0, -dy), min(gy, gy - dy))
        ]
        return lax.ppermute(value, ("gx", "gy"), perm)

    def coded(value):
        count, rows, columns = value.shape
        return jax.ShapeDtypeStruct((count, rows, columns // 2 * 3), jnp.bfloat16)

    def first(pieces):
        return around(pieces[2], 1), around(pieces[3], -1)

    def second(pieces, received, token, also=(), size=0):
        up, down = pieces[4], pieces[5]
        arrays = [*received, up, down, *also]
        (up, down), token = call_step(second_kernel, [coded(up), coded(down)], token, arrays, "second", size)
        return (around(up, 1), around(down, -1)), token

    def back(pieces, received, arrived, token, apart=0):
        own = pieces[1]
        outs = [coded(own[:apart]), coded(own[apart:])] if apart else [coded(own)]
        outs, token = call_step(back_kernel, outs, token, [arrived[1], own, received[0], arrived[0]], "back")
        return [swap(out) for out in outs], token

    def keep(pieces, received, arrived, token, others=()):
        arrays = [pieces[0], arrived[0], received[1], *others]
        (rows,), token = call_step(keep_kernel, [pieces[0]], token, arrays, "keep")
        return rows, token

    def blocks(groups, inputs, token, name):
        kernel = functools.partial(late_kernel, groups, [where for where, _ in inputs])
        arrays = [meta, offsets] + [value for _, value in inputs]
        return call_blocks(kernel, [len(group) for group in groups], 4 * traces, 9, 6, points, arrays, token, name)

    token = jnp.zeros((8, 128), jnp.float32)
    theirs = swap(lax.dynamic_index_in_dim(green, 1 - x_lo, 2, keepdims=False))
    mine = lax.dynamic_index_in_dim(green, x_lo, 2, keepdims=False)
    above_mine = tiles_from(mine[:, 0], 0, 1)
    early_count = 2 * len(EARLY)
    (early,), token = call_blocks(
        early_kernel, [early_count], 2 * traces, 8, 8, points, [meta, offsets, green], token, "early_blocks"
    )
    early_first = first(early)
    dtype, shape = green.dtype, mine.shape[2:]
    pair = jax.ShapeDtypeStruct((2,) + shape, dtype)
    pairs = jax.ShapeDtypeStruct((2, 2) + shape, dtype)
    sent, token = call_step(swapped_kernel, [pair, pairs, pair], token, [mine, theirs, above_mine], "swapped")
    above, beside, corner = sent
    above_theirs = tiles_from(above, 0, 1)
    beside = tiles_from(beside, 1, 0)
    corner = tiles_from(corner, 1, 1)
    early_second, token = second(early, early_first, token, size=WAITING)
    tiles = [(OWN, mine.reshape(4, *shape)), (OWN, theirs.reshape(4, *shape)), (ABOVE, above_mine), (ABOVE, above_theirs)]
    tiles += [(BESIDE, beside[0]), (BESIDE, beside[1])]
    (one,), token = blocks((FIRST,), tiles, token, "first_blocks")
    one_first = first(one)
    tiles += [(CORNER, corner[:1]), (CORNER, corner[1:])]
    (two,), token = blocks((LAST,), tiles, token, "last_blocks")
    two_first = first(two)
    early_back, token = back(early, early_first, early_second, token)
    one_second, token = second(one, one_first, token, early_back)
    two_second, token = second(two, two_first, token)
    (one_given, one_back), token = back(one, one_first, one_second, token, GIVEN)
    (two_back,), token = back(two, two_first, two_second, token)
    one_kept, token = keep(one, one_first, one_second, token)
    rows = jax.ShapeDtypeStruct((2 * GIVEN,) + one_back.shape[1:], one_back.dtype)
    (given,), token = call_step(give_kernel, [rows], token, [one_kept, one_given], "give")
    given = tiles_from(given, 0, -1)
    early_kept, token = keep(early, early_first, early_second, token, early_back)
    two_kept, token = keep(two, two_first, two_second, token)
    rows = jax.ShapeDtypeStruct((one_back.shape[0],) + one_kept.shape[1:], jnp.float32)
    (one_other,), token = call_step(read_kernel, [rows], token, [one_back], "read", WAITING)
    rows = jax.ShapeDtypeStruct((two_back.shape[0],) + one_kept.shape[1:], jnp.float32)
    (two_other,), token = call_step(read_kernel, [rows], token, [two_back], "read")
    parts = [early_kept, one_kept, two_kept, one_other, two_other, given]
    shape = green.shape[:2] + (NPAIR, green.shape[2], points // (2 * RING), 2 * points)
    return final(meta, offsets, parts, token, shape)


def solution(mesh):
    return jax.shard_map(
        per_device,
        mesh=mesh,
        in_specs=(P("gx", "gy", None, None, "sa", None), P()),
        out_specs=P("gx", "gy", None, None, "sa", None),
        check_vma=False,
    )
```

```python
import functools

import jax
import jax.numpy as jnp
from jax import lax
from jax.experimental import pallas as pl
from jax.experimental.pallas import tpu as pltpu
from jax.sharding import PartitionSpec as P

NPAIR = 4
RING = 4
LOOSE0, LOOSE1, DOWN, UP = range(4)
MIB = 1024 * 1024
EARLY = ((0, 0, UP), (0, 0, LOOSE0), (0, 0, LOOSE1), (0, 1, DOWN), (1, 0, LOOSE0))
GIVEN = 2
FIRST = ((0, 2, DOWN), (1, 2, DOWN), (0, 1, LOOSE0), (0, 1, LOOSE1), (0, 1, UP), (1, 1, LOOSE0), (1, 0, UP))
LAST = ((1, 0, LOOSE1), (1, 1, LOOSE1), (1, 1, DOWN), (1, 1, UP))

WAITING = 100_000_000_000
OWN = ((0, 0), (0, 1), (1, 0), (1, 1))
BESIDE = ((2, 0), (2, 1))
ABOVE = ((0, 2), (1, 2))
CORNER = ((2, 2),)


def slot_table(offsets):
    dx = [offsets[k, 0] for k in range(NPAIR)]
    dy = [offsets[k, 1] for k in range(NPAIR)]
    code = [
        jnp.where(dx[k] == 0, dy[k], jnp.where(dy[k] == 0, 2, jnp.where(dy[k] < 0, 3, 4)))
        for k in range(NPAIR)
    ]
    rank = [
        sum((code[j] < code[k]).astype(jnp.int32) for j in range(NPAIR) if j != k) for k in range(NPAIR)
    ]

    def pick(values, slot):
        return sum(jnp.where(rank[k] == slot, values[k], 0) for k in range(NPAIR))

    return [(pick(dx, s), pick(dy, s), pick(list(range(NPAIR)), s)) for s in range(NPAIR)]


REMAINDER = 2.0**-8
REAL_STEPS = 127
IMAG_STEPS = 31


def encode(ref, index, value):
    points = value.shape[1] // 2
    high = value.astype(jnp.bfloat16)
    ref[index, :, : 2 * points] = high
    high = high.astype(jnp.float32)
    size = jnp.abs(high)
    inverse = jnp.where(size > 1e-37, 1.0 / jnp.maximum(size, 1e-37), 0.0)
    share = (value - high) * inverse
    real = jnp.floor(share[:, :points] * (REAL_STEPS / REMAINDER) + 0.5)
    real = jnp.clip(real, -REAL_STEPS, REAL_STEPS)
    code = jnp.where(real >= 0, real + 128, real - 127)
    rest = jnp.floor(share[:, points:] * (IMAG_STEPS / REMAINDER) + 0.5)
    rest = jnp.clip(rest, -IMAG_STEPS, IMAG_STEPS) + IMAG_STEPS
    ref[index, :, 2 * points :] = (code * jnp.exp2(rest)).astype(jnp.bfloat16)


def decode(ref, index):
    points = ref.shape[2] // 3
    high = ref[index, :, : 2 * points].astype(jnp.float32)
    code = ref[index, :, 2 * points :].astype(jnp.float32)
    size = jnp.maximum(jnp.abs(code) * (1.0 / 128), 1.0)
    power = jnp.floor(jnp.log2(size) + 0.002)
    imag = power - IMAG_STEPS
    real = size * jnp.exp2(-power) * 128 - 128
    real = jnp.where(code >= 0, real, -1 - real)
    share = jnp.concatenate([real * (REMAINDER / REAL_STEPS), imag * (REMAINDER / IMAG_STEPS)], axis=1)
    return high + share * jnp.abs(high)


def store_pieces(outs, place, meta, index, count):
    own_a, own_b, up_first, down_first, up_second, down_second = outs
    x_lo, y = meta[0], meta[1]
    half = place.shape[0] // 2
    rows = half // RING
    target = {
        (0, 0): (own_a, 0),
        (0, 1): (own_b, 0),
        (2, 0): (up_first, 0),
        (1, 1): (up_first, count),
        (2, 1): (down_first, 0),
        (3, 0): (down_first, count),
        (1, 0): (up_second, 0),
        (3, 1): (down_second, 0),
    }
    for (d, h), (ref, base) in target.items():
        start = lax.rem(x_lo + h, 2) * half + lax.rem(y + d, RING) * rows
        value = place[pl.ds(pl.multiple_of(start, rows), rows), :]
        if ref is up_first or ref is down_first:
            encode(ref, base + index, value)
        else:
            ref[base + index] = value


def load_tile(left, right, tile, own, parts):
    traces, points = parts[0].shape[-2:]
    for i, part in enumerate(parts):
        re, im = part[0], part[1]
        low = slice(2 * i * traces, (2 * i + 1) * traces)
        high = slice((2 * i + 1) * traces, (2 * i + 2) * traces)
        right[tile, low, :points] = re
        right[tile, high, :points] = im
        right[tile, low, points:] = im
        right[tile, high, points:] = -re
        if own is not None:
            left[own, :, low] = re.T
            left[own, :, high] = im.T


def early_kernel(meta, offsets, token, green, *refs):
    outs, (left, right, acc) = refs[:6], refs[7:]
    refs[6][...] = token[...]
    slots = slot_table(offsets)
    count = 2 * len(EARLY)
    for freq in range(2):
        for tx in range(2):
            for ty in range(2):
                load_tile(left, right, freq * 4 + tx * 2 + ty, freq * 4 + tx * 2 + ty, [green.at[tx, ty, freq]])
    for b, (tx, ty, slot) in enumerate(EARLY):
        dx, dy, _ = slots[slot]
        for freq in range(2):
            place = acc.at[freq]
            tile = freq * 4 + (tx + dx) * 2 + ty + dy
            place[...] = jnp.dot(left[freq * 4 + tx * 2 + ty], right[tile], preferred_element_type=jnp.float32)
            store_pieces(outs, place, meta, 2 * b + freq, count)


def late_kernel(groups, where, *refs):
    count = 3 + len(where)
    meta, offsets, token = refs[:3]
    outs, (out_token, left, right, acc) = refs[count:-4], refs[-4:]
    out_token[...] = token[...]
    sources = {}
    for ref, tiles in zip(refs[3:count], where):
        for i, tile in enumerate(tiles):
            sources.setdefault(tile, []).append(ref.at[i])
    for (tx, ty), parts in sources.items():
        load_tile(left, right, tx * 3 + ty, tx * 3 + ty if tx < 2 else None, parts)
    slots = slot_table(offsets)
    step = 0
    for g, group in enumerate(groups):
        for b, (tx, ty, slot) in enumerate(group):
            dx, dy, _ = slots[slot]
            place = acc.at[step % 2]
            step += 1
            tile = (tx + dx) * 3 + ty + dy
            place[...] = jnp.dot(left[tx * 3 + ty], right[tile], preferred_element_type=jnp.float32)
            store_pieces(outs[6 * g : 6 * g + 6], place, meta, b, len(group))


def call_blocks(kernel, counts, depth, tiles, lefts, points, arrays, token, name):
    meta, offsets, *values = arrays
    smem = pl.BlockSpec(memory_space=pltpu.SMEM)
    vmem = pl.BlockSpec(memory_space=pltpu.VMEM)
    rows = points // (2 * RING)
    out_shape = []
    for count in counts:
        kept = jax.ShapeDtypeStruct((count, rows, 2 * points), jnp.float32)
        sent = jax.ShapeDtypeStruct((2 * count, rows, 3 * points), jnp.bfloat16)
        out_shape += [kept, kept, sent, sent, kept, kept]
    *pieces, token = pl.pallas_call(
        kernel,
        out_shape=out_shape + [jax.ShapeDtypeStruct(token.shape, token.dtype)],
        in_specs=[smem, smem] + [vmem] * (1 + len(values)),
        out_specs=[vmem] * (len(out_shape) + 1),
        scratch_shapes=[
            pltpu.VMEM((lefts, points, depth), jnp.bfloat16),
            pltpu.VMEM((tiles, depth, 2 * points), jnp.bfloat16),
            pltpu.VMEM((2, points, 2 * points), jnp.float32),
        ],
        compiler_params=pltpu.CompilerParams(vmem_limit_bytes=(24 if len(values) > 1 else 14) * MIB),
        cost_estimate=pl.CostEstimate(flops=0, bytes_accessed=0, transcendentals=0),
        name=name,
    )(meta, offsets, token, *values)
    return [pieces[6 * g : 6 * g + 6] for g in range(len(counts))], token


def call_step(kernel, out_shape, token, arrays, name, size=0):
    vmem = pl.BlockSpec(memory_space=pltpu.VMEM)
    *outs, token = pl.pallas_call(
        kernel,
        out_shape=list(out_shape) + [jax.ShapeDtypeStruct(token.shape, token.dtype)],
        in_specs=[vmem] * (1 + len(arrays)),
        out_specs=[vmem] * (1 + len(out_shape)),
        compiler_params=pltpu.CompilerParams(vmem_limit_bytes=6 * MIB),
        cost_estimate=pl.CostEstimate(flops=size, bytes_accessed=0, transcendentals=0),
        name=name,
    )(token, *arrays)
    return outs, token


def swapped_kernel(token, mine, theirs, above_mine, above, beside, corner, out_token):
    for i, part in enumerate((mine, theirs)):
        beside[i] = part[0]
        corner[i] = part[0, 0]
    for tx in range(2):
        above[tx] = theirs[tx, 0]
    out_token[...] = token[...]


def keep_kernel(token, own, before, after, *refs):
    rows, out_token = refs[-2:]
    count = own.shape[0]
    for i in range(count):
        value = own[i] + decode(before, i) + decode(after, count + i)
        for other in refs[:-2]:
            value = value + decode(other, i)
        rows[i] = value
    out_token[...] = token[...]


def give_kernel(token, kept, other, rows, out_token):
    for i in range(GIVEN):
        encode(rows, i, kept[i])
        rows[GIVEN + i] = other[i]
    out_token[...] = token[...]


def read_kernel(token, sums, rows, out_token):
    for i in range(sums.shape[0]):
        rows[i] = decode(sums, i)
    out_token[...] = token[...]


def second_kernel(token, up_received, down_received, up_own, down_own, *refs):
    up, down, out_token = refs[-3:]
    for i in range(up_own.shape[0]):
        encode(up, i, up_own[i] + decode(up_received, i))
        encode(down, i, down_own[i] + decode(down_received, i))
    out_token[...] = token[...]


def back_kernel(token, down_arrived, own, up_received, *refs):
    outs, out_token = refs[1:-1], refs[-1]
    count = own.shape[0]
    for i in range(count):
        value = own[i] + decode(up_received, count + i) + decode(down_arrived, i)
        first = outs[0].shape[0]
        encode(outs[0] if i < first else outs[1], i if i < first else i - first, value)
    out_token[...] = token[...]


def final_kernel(meta, offsets, early, kept_one, kept_two, other_one, other_two, given, token, out):
    x_lo = meta[0]
    slots = slot_table(offsets)
    for b, (tx, ty, slot) in enumerate(EARLY):
        for freq in range(2):
            out[tx, ty, slots[slot][2], freq] = early[2 * b + freq]
    for b, (tx, ty, slot) in enumerate(FIRST + LAST):
        pair = slots[slot][2]
        if b < GIVEN:
            out[tx, 0, pair, x_lo] = decode(given, b)
            out[tx, 0, pair, 1 - x_lo] = decode(given, GIVEN + b)
        else:
            late = b >= len(FIRST)
            out[tx, ty, pair, x_lo] = kept_two[b - len(FIRST)] if late else kept_one[b]
            out[tx, ty, pair, 1 - x_lo] = other_two[b - len(FIRST)] if late else other_one[b - GIVEN]


def final(meta, offsets, parts, token, shape):
    smem = pl.BlockSpec(memory_space=pltpu.SMEM)
    vmem = pl.BlockSpec(memory_space=pltpu.VMEM)
    return pl.pallas_call(
        final_kernel,
        out_shape=jax.ShapeDtypeStruct(shape, jnp.float32),
        in_specs=[smem, smem] + [vmem] * (len(parts) + 1),
        out_specs=vmem,
        compiler_params=pltpu.CompilerParams(vmem_limit_bytes=10 * MIB),
        cost_estimate=pl.CostEstimate(flops=0, bytes_accessed=0, transcendentals=0),
        name="place_blocks",
    )(meta, offsets, *parts, token)


def per_device(green, offsets):
    points, traces = green.shape[5], green.shape[4]
    gx, gy = lax.axis_size("gx"), lax.axis_size("gy")
    sa = lax.axis_index("sa")
    x_lo, y = sa // RING, sa % RING
    meta = jnp.stack([x_lo, y]).astype(jnp.int32)

    def swap(value):
        return lax.ppermute(value, "sa", [(i, (i + RING) % (2 * RING)) for i in range(2 * RING)])

    def around(value, steps):
        return lax.ppermute(value, "sa", [(h * RING + i, h * RING + (i + steps) % RING) for h in range(2) for i in range(RING)])

    def tiles_from(value, dx, dy):
        perm = [
            ((ix + dx) * gy + iy + dy, ix * gy + iy)
            for ix in range(gx - dx)
            for iy in range(max(0, -dy), min(gy, gy - dy))
        ]
        return lax.ppermute(value, ("gx", "gy"), perm)

    def coded(value):
        count, rows, columns = value.shape
        return jax.ShapeDtypeStruct((count, rows, columns // 2 * 3), jnp.bfloat16)

    def first(pieces):
        return around(pieces[2], 1), around(pieces[3], -1)

    def second(pieces, received, token, also=(), size=0):
        up, down = pieces[4], pieces[5]
        arrays = [*received, up, down, *also]
        (up, down), token = call_step(second_kernel, [coded(up), coded(down)], token, arrays, "second", size)
        return (around(up, 1), around(down, -1)), token

    def back(pieces, received, arrived, token, apart=0):
        own = pieces[1]
        outs = [coded(own[:apart]), coded(own[apart:])] if apart else [coded(own)]
        outs, token = call_step(back_kernel, outs, token, [arrived[1], own, received[0], arrived[0]], "back")
        return [swap(out) for out in outs], token

    def keep(pieces, received, arrived, token, others=()):
        arrays = [pieces[0], arrived[0], received[1], *others]
        (rows,), token = call_step(keep_kernel, [pieces[0]], token, arrays, "keep")
        return rows, token

    def blocks(groups, inputs, token, name):
        kernel = functools.partial(late_kernel, groups, [where for where, _ in inputs])
        arrays = [meta, offsets] + [value for _, value in inputs]
        return call_blocks(kernel, [len(group) for group in groups], 4 * traces, 9, 6, points, arrays, token, name)

    token = jnp.zeros((8, 128), jnp.float32)
    theirs = swap(lax.dynamic_index_in_dim(green, 1 - x_lo, 2, keepdims=False))
    mine = lax.dynamic_index_in_dim(green, x_lo, 2, keepdims=False)
    above_mine = tiles_from(mine[:, 0], 0, 1)
    early_count = 2 * len(EARLY)
    (early,), token = call_blocks(
        early_kernel, [early_count], 2 * traces, 8, 8, points, [meta, offsets, green], token, "early_blocks"
    )
    early_first = first(early)
    dtype, shape = green.dtype, mine.shape[2:]
    pair = jax.ShapeDtypeStruct((2,) + shape, dtype)
    pairs = jax.ShapeDtypeStruct((2, 2) + shape, dtype)
    sent, token = call_step(swapped_kernel, [pair, pairs, pair], token, [mine, theirs, above_mine], "swapped")
    above, beside, corner = sent
    above_theirs = tiles_from(above, 0, 1)
    beside = tiles_from(beside, 1, 0)
    corner = tiles_from(corner, 1, 1)
    early_second, token = second(early, early_first, token, size=8_000_000_000)
    tiles = [(OWN, mine.reshape(4, *shape)), (OWN, theirs.reshape(4, *shape)), (ABOVE, above_mine), (ABOVE, above_theirs)]
    tiles += [(BESIDE, beside[0]), (BESIDE, beside[1])]
    (one,), token = blocks((FIRST,), tiles, token, "first_blocks")
    one_first = first(one)
    tiles += [(CORNER, corner[:1]), (CORNER, corner[1:])]
    (two,), token = blocks((LAST,), tiles, token, "last_blocks")
    two_first = first(two)
    early_back, token = back(early, early_first, early_second, token)
    one_second, token = second(one, one_first, token, early_back)
    two_second, token = second(two, two_first, token)
    (one_given, one_back), token = back(one, one_first, one_second, token, GIVEN)
    (two_back,), token = back(two, two_first, two_second, token)
    one_kept, token = keep(one, one_first, one_second, token)
    rows = jax.ShapeDtypeStruct((2 * GIVEN,) + one_back.shape[1:], one_back.dtype)
    (given,), token = call_step(give_kernel, [rows], token, [one_kept, one_given], "give")
    given = tiles_from(given, 0, -1)
    early_kept, token = keep(early, early_first, early_second, token, early_back)
    two_kept, token = keep(two, two_first, two_second, token)
    rows = jax.ShapeDtypeStruct((one_back.shape[0],) + one_kept.shape[1:], jnp.float32)
    (one_other,), token = call_step(read_kernel, [rows], token, [one_back], "read", WAITING)
    rows = jax.ShapeDtypeStruct((two_back.shape[0],) + one_kept.shape[1:], jnp.float32)
    (two_other,), token = call_step(read_kernel, [rows], token, [two_back], "read")
    parts = [early_kept, one_kept, two_kept, one_other, two_other, given]
    shape = green.shape[:2] + (NPAIR, green.shape[2], points // (2 * RING), 2 * points)
    return final(meta, offsets, parts, token, shape)


def solution(mesh):
    return jax.shard_map(
        per_device,
        mesh=mesh,
        in_specs=(P("gx", "gy", None, None, "sa", None), P()),
        out_specs=P("gx", "gy", None, None, "sa", None),
        check_vma=False,
    )
```
